32 devices in a mesh: blk: 32 (over z, y, x, core), seq: 1, mp: 1.
Axes of the slice: x: 2, y: 2, z: 4, core: 2. Of those that a mesh axis runs over, the one named last changes fastest.
Arguments:
- hidden: bfloat16 [1, 512, 1536], P(('mp', 'seq'), 'blk'), may hold values from -6 to 6
- labels: int32 [1, 512], P('seq'), may hold values from 0 to 25151
- lengths: int32 [1, 8], P('seq'), may hold values from 1 to 256, 512 in all within a row
- owners: int32 [8], replicated, may hold values from 0 to 7, each once
- w_inner: bfloat16 [1536, 2, 1536], P('mp', None, 'blk'), may hold values from -0.15625 to 0.15625
- w_bcdt: bfloat16 [1536, 280], P('mp'), may hold values from -0.15625 to 0.15625
- conv_inner: float32 [4, 1536], P('mp', 'blk'), may hold values from -3 to 3
- conv_bc: float32 [4, 256], P('mp'), may hold values from -3 to 3
- dt_bias: float32 [24], P('mp'), may hold values from -3 to 0.5
- decay_rate: float32 [24], P('mp'), may hold values from 0.01 to 1
- d_skip: float32 [24], P('mp'), may hold values from 0.5 to 2
- norm_gain: float32 [1536], P(('mp', 'blk')), may hold values from 0.5 to 1.5
- w_out: bfloat16 [1536, 1536], P(('mp', 'blk')), may hold values from -0.15625 to 0.15625
- final_gain: float32 [1536], P('mp'), may hold values from 0.5 to 1.5
- w_head: bfloat16 [1536, 25152], P('mp', 'blk'), may hold values from -0.33170174 to 0.33170174
Outputs:
- layer_out: bfloat16 [1, 512, 1536], P(('mp', 'seq'), 'blk')
- token_logprob: float32 [1, 512], P(('mp', 'seq'), 'blk')
- seq_logprob: float32 [8], P(('mp', 'seq'))
The draws below stay inside these ranges and needn't reach their ends.
Inputs may be any that keep to these rules, and one draw needn't show every extreme that they name: The 8 lengths of a group sum to 512 and the longest is exactly 256. `owners`: every output slot is named once.
All inputs are finite; a program needn't handle non-finite values.
Results may differ from the reference program's by a relative error of at most 0.0055.
Values may be sent and summed in bfloat16 or wider, within the bound.
A program may use at most 64 MiB of HBM per device.

```python
import math
import jax
import jax.numpy as jnp
import numpy as np
from jax import lax

D = 1536
HEADDIM = 64
NSTATE = 128
CONV = 4
T_SEQ = 512
SEQS = 8
INNER = 1536
HEADS = 24
VOCAB = 25152
LONG = 256
GROUPS = 1


def draw_hidden(key, part):
    shape = (GROUPS, T_SEQ, D)
    values = jnp.clip(jax.random.normal(jax.random.fold_in(key, 10), shape, jnp.float32), -6.0, 6.0)
    return values.astype(jnp.bfloat16)


def draw_w_head(key, part):
    shape = (D, VOCAB)
    spread_scale = 3.2 / math.sqrt(D)
    values = jnp.clip(jax.random.normal(jax.random.fold_in(key, 20), shape, jnp.float32), -4.0, 4.0) * spread_scale
    return values.astype(jnp.bfloat16)


def with_ends(values, stream_key, smallest, largest):
    longest = values.shape.index(max(values.shape))
    spots = []
    for shift in (0, 1):
        where = [jax.random.randint(jax.random.fold_in(stream_key, axis), (), 0, length) for axis, length in enumerate(values.shape)]
        where[longest] = (where[longest] + shift) % values.shape[longest]
        spots.append(tuple(where))
    return values.at[spots[0]].set(smallest).at[spots[1]].set(largest)


def level_of(key, extent, pieces, low, top_value):
    def one(dim, shards_of):
        heights = jax.random.uniform(jax.random.fold_in(jax.random.fold_in(key, 6), dim), (shards_of,), jnp.float32, low / len(pieces), top_value / len(pieces))
        return jnp.repeat(jnp.exp(heights), extent[dim] // shards_of).reshape((-1,) + (1,) * (len(extent) - dim - 1))

    level = one(*pieces[0])
    for cut in pieces[1:]:
        level = level * one(*cut)
    return level


def rank_table(amount, lean):
    portions = [(1 << 20) // math.isqrt(grade ** lean) + 1 for grade in range(1, amount + 1)]
    scale = 1 + sum(portions) // (1 << 30)
    return np.cumsum(np.array([max(1, weight // scale) for weight in portions]))


def ranked_ids(stream_key, extent, number_of, lean):
    table = rank_table(number_of, lean)
    ticket = jax.random.randint(jax.random.fold_in(stream_key, 1), extent, 0, int(table[number_of - 1]))
    grade = jnp.searchsorted(jnp.asarray(table, jnp.int32), ticket, side="right")
    return jax.random.permutation(jax.random.fold_in(stream_key, 2), number_of)[grade].astype(jnp.int32)


def profile(amount, total, bound, lean):
    weights = [(1 << 20) // math.isqrt(standing ** lean) + 1 for standing in range(2, amount + 1)]
    spare, given = total - bound - (amount - 1), [1] * (amount - 1)
    while spare > 0:
        free = [i for i in range(amount - 1) if given[i] < bound]
        pool, left = sum([weights[i] for i in free]), spare
        for i in free:
            more = min(bound - given[i], max(1, left * weights[i] // pool), spare)
            given[i] = given[i] + more
            spare = spare - more
    return np.array([bound] + given)


def uneven_parts(stream_key, count, total, most, skew):
    if count == 2:
        one = jax.random.randint(stream_key, (), max(1, total - most), min(most, total - 1) + 1)
        return jnp.stack([one, total - one])
    sizes = jnp.asarray(profile(count, total, most, skew), jnp.int32)
    couples = (count - 1) // 2
    source_of, taker = sizes[1:1 + 2 * couples:2], sizes[2:2 + 2 * couples:2]
    room = jnp.minimum(source_of - 1, most - taker)
    shifted = jax.random.randint(jax.random.fold_in(stream_key, 1), (couples,), 0, 1 << 20) % (room + 1)
    sizes = sizes.at[1:1 + 2 * couples:2].set(source_of - shifted).at[2:2 + 2 * couples:2].set(taker + shifted)
    return sizes[jax.random.permutation(jax.random.fold_in(stream_key, 2), count)]


def normal_values(stream_key, dims, deviation, bound, pieces=(), kind=jnp.bfloat16):
    factor_of = level_of(stream_key, dims, pieces, -0.22, 0.18) if pieces else 1.0
    entries = jax.random.normal(stream_key, dims, jnp.float32) * deviation * factor_of
    return jnp.minimum(jnp.maximum(entries, -bound), bound).astype(kind)


def setup_inputs(seed: int = 0, part: int = 0) -> dict:
    key_list = jax.random.split(jax.random.key(seed), 16)
    part_keys = jax.random.split(jax.random.fold_in(key_list[15], part), 16)
    return {
        "hidden": draw_hidden(jax.random.fold_in(jax.random.fold_in(key_list[15], part), 71), part),
        "labels": with_ends(ranked_ids(key_list[1], (GROUPS, T_SEQ), VOCAB, 2), jax.random.fold_in(key_list[1], 3), 0, VOCAB - 1).astype(jnp.int32),
        "lengths": jax.vmap(lambda own: uneven_parts(own, SEQS, T_SEQ, LONG, 2))(jax.random.split(key_list[2], GROUPS)).reshape((GROUPS, SEQS)).astype(jnp.int32),
        "owners": jax.random.permutation(key_list[3], GROUPS * SEQS).astype(jnp.int32),
        "w_inner": normal_values(part_keys[4], (D, 2, INNER), D ** -0.5, 0.15625, ((2, 32),)),
        "w_bcdt": normal_values(part_keys[5], (D, 2 * NSTATE + HEADS), D ** -0.5, 0.15625),
        "conv_inner": normal_values(part_keys[6], (CONV, INNER), CONV ** -0.5, 3.0, ((1, 32),), jnp.float32),
        "conv_bc": normal_values(part_keys[7], (CONV, 2 * NSTATE), CONV ** -0.5, 3.0, (), jnp.float32),
        "dt_bias": jnp.clip(jax.random.uniform(part_keys[8], (HEADS,), jnp.float32, -3.0, 0.5), -3.0, 0.5),
        "decay_rate": jnp.clip(jnp.exp(jax.random.uniform(part_keys[9], (HEADS,), jnp.float32, math.log(0.01), math.log(1.0))), 0.01, 1.0),
        "d_skip": jnp.clip(jax.random.uniform(part_keys[10], (HEADS,), jnp.float32, 0.5, 2.0), 0.5, 2.0),
        "norm_gain": jnp.clip(1.0 + 0.1 * jax.random.normal(part_keys[11], (INNER,), jnp.float32), 0.5, 1.5),
        "w_out": normal_values(part_keys[12], (INNER, D), INNER ** -0.5, 0.15625, ((0, 32),)),
        "final_gain": jnp.clip(1.0 + 0.1 * jax.random.normal(part_keys[13], (D,), jnp.float32), 0.5, 1.5),
        "w_head": draw_w_head(jax.random.fold_in(jax.random.fold_in(key_list[15], part), 71), part),
    }


EPSILON = 1e-05
HIGH = lax.Precision.HIGHEST

def segments_of(lengths):
    starts = jnp.cumsum(lengths, axis=-1) - lengths
    places = jnp.arange(T_SEQ, dtype=jnp.int32)
    segment = lax.optimization_barrier(jnp.sum((places[:, None] >= starts[..., None, :]).astype(jnp.int32), axis=-1)) - 1
    first = jnp.take_along_axis(starts, segment, axis=-1)
    return (segment, places - first)

def causal_conv(values, weights, position):
    total = values * weights[0]
    for shift_by in range(1, CONV):
        moved = jnp.concatenate([jnp.zeros_like(values[..., :shift_by, :]), values[..., :-shift_by, :]], axis=-2)
        total = total + moved * weights[shift_by] * (position >= shift_by).astype(jnp.float32)[..., None]
    return total

def final_norm(values, gain):
    widened = values.astype(jnp.float32)
    scale = lax.rsqrt(lax.optimization_barrier(jnp.mean(widened * widened, axis=-1, keepdims=True)) + EPSILON)
    return (widened * scale * gain).astype(jnp.bfloat16)

def time_major(array):
    return jnp.swapaxes(array, 0, 1)

def reference(hidden, labels, lengths, owners, w_inner, w_bcdt, conv_inner, conv_bc, dt_bias, decay_rate, d_skip, norm_gain, w_out, final_gain, w_head):
    flat = hidden.reshape(GROUPS * T_SEQ, D)
    inner_proj = jnp.dot(flat, w_inner.reshape(D, 2 * INNER), preferred_element_type=jnp.float32).astype(jnp.bfloat16)
    inner_proj = inner_proj.reshape(GROUPS, T_SEQ, 2 * INNER)
    state_proj = jnp.dot(flat, w_bcdt, preferred_element_type=jnp.float32).astype(jnp.bfloat16)
    state_proj = state_proj.reshape(GROUPS, T_SEQ, 2 * NSTATE + HEADS)
    gate_half = inner_proj[..., :INNER].astype(jnp.float32)
    segment, position = segments_of(lengths)
    conv_value = jax.nn.silu(causal_conv(inner_proj[..., INNER:].astype(jnp.float32), conv_inner, position))
    conv_state = jax.nn.silu(causal_conv(state_proj[..., :2 * NSTATE].astype(jnp.float32), conv_bc, position))
    input_map = conv_state[..., :NSTATE]
    output_map = conv_state[..., NSTATE:]
    step_size = jax.nn.softplus(state_proj[..., 2 * NSTATE:].astype(jnp.float32) + dt_bias)
    channel_head = jnp.arange(INNER) // HEADDIM
    log_decay = -(step_size * decay_rate)[..., channel_head]
    driven = conv_value * step_size[..., channel_head]
    keep = (position > 0).astype(jnp.float32)

    def advance(carried, inputs):
        decay_now, drive_now, in_now, out_now, keep_now = inputs
        factor = jnp.exp(decay_now) * keep_now[:, None]
        carried = carried * factor[:, :, None] + drive_now[:, :, None] * in_now[:, None, :]
        return (carried, lax.optimization_barrier(jnp.sum(carried * out_now[:, None, :], axis=-1)))
    initial = jnp.zeros((GROUPS, INNER, NSTATE), jnp.float32)
    final_state, scanned = lax.scan(advance, initial, (time_major(log_decay), time_major(driven), time_major(input_map), time_major(output_map), time_major(keep)))
    mixed = time_major(scanned) + d_skip[channel_head] * conv_value
    gated = mixed * jax.nn.silu(gate_half)
    scale = lax.rsqrt(lax.optimization_barrier(jnp.mean(gated * gated, axis=-1, keepdims=True)) + EPSILON)
    gated_norm = (gated * scale * norm_gain).astype(jnp.bfloat16).reshape(GROUPS * T_SEQ, INNER)
    delta = jnp.dot(gated_norm, w_out, preferred_element_type=jnp.float32)
    layer_out = (flat.astype(jnp.float32) + delta).astype(jnp.bfloat16)
    normed = final_norm(layer_out, final_gain).reshape(GROUPS, T_SEQ, D)

    def score(rows):
        normed_rows, label_rows = rows
        logits = jnp.dot(normed_rows, w_head, preferred_element_type=jnp.float32)
        total = jax.nn.logsumexp(logits, axis=-1)
        target = jnp.take_along_axis(logits, label_rows[:, None], axis=-1)[:, 0]
        return target - total
    token_logprob = lax.map(score, (normed, labels))
    onehot = (segment[..., None] == jnp.arange(SEQS, dtype=jnp.int32)).astype(jnp.float32)
    sums = jnp.einsum('gt,gts->gs', token_logprob, onehot, precision=HIGH)
    seq_logprob = jnp.zeros((GROUPS * SEQS,), jnp.float32).at[owners].set(sums.reshape(-1))
    return (layer_out.reshape(GROUPS, T_SEQ, D), token_logprob, seq_logprob)
```

```python
import functools

import jax
import jax.numpy as jnp
from jax import lax
from jax.experimental import pallas as pl
from jax.experimental.pallas import tpu as pltpu
from jax.sharding import PartitionSpec as P

D = 1536
HEADDIM = 64
NSTATE = 128
SCAN_BLOCK = 256
CONV = 4


EPSILON = 1e-05
HIGH = lax.Precision.HIGHEST


def segments_of(lengths, count):
    order = jnp.arange(lengths.shape[0], dtype=jnp.int32)
    earlier = order[None, :] < order[:, None]
    starts = jnp.sum(jnp.where(earlier, lengths[None, :], 0), axis=-1)
    places = jnp.arange(count, dtype=jnp.int32)
    segment = jnp.sum((places[:, None] >= starts[None, :]).astype(jnp.int32), axis=-1) - 1
    first = jnp.take(starts, segment)
    return (segment, places - first)


def causal_conv(values, weights, position):
    total = values * weights[0]
    for shift_by in range(1, CONV):
        moved = jnp.concatenate(
            [jnp.zeros_like(values[:shift_by, :]), values[:-shift_by, :]], axis=0
        )
        total = (
            total + moved * weights[shift_by] * (position >= shift_by).astype(jnp.float32)[:, None]
        )
    return total


def final_norm(values, gain):
    widened = values.astype(jnp.float32)
    scale = lax.rsqrt(jnp.mean(widened * widened, axis=-1, keepdims=True) + EPSILON)
    return (widened * scale * gain).astype(jnp.bfloat16)


def shards(
    hidden,
    labels,
    lengths,
    owners,
    w_inner,
    w_bcdt,
    conv_inner,
    conv_bc,
    dt_bias,
    decay_rate,
    d_skip,
    norm_gain,
    w_out,
    final_gain,
    w_head,
):
    rows_own = hidden[0]
    rows_count = rows_own.shape[0]
    blk_count = lax.axis_size("blk")
    blk_index = lax.axis_index("blk")
    gathered = lax.all_gather(rows_own, "blk", axis=0, tiled=True)
    tokens_all = gathered.shape[0]
    channels = w_inner.shape[2]
    inner_total = channels * blk_count
    inner_proj = jnp.dot(
        gathered, w_inner.reshape(D, 2 * channels), preferred_element_type=jnp.float32
    ).astype(jnp.bfloat16)
    state_proj = jnp.dot(gathered, w_bcdt, preferred_element_type=jnp.float32).astype(jnp.bfloat16)
    gate_half = inner_proj[:, :channels].astype(jnp.float32)
    segment, position = segments_of(lengths[0], tokens_all)
    conv_value = jax.nn.silu(
        causal_conv(inner_proj[:, channels:].astype(jnp.float32), conv_inner, position)
    )
    conv_state = jax.nn.silu(
        causal_conv(state_proj[:, : 2 * NSTATE].astype(jnp.float32), conv_bc, position)
    )
    input_map = conv_state[:, :NSTATE]
    output_map = conv_state[:, NSTATE:]
    step_size = jax.nn.softplus(state_proj[:, 2 * NSTATE :].astype(jnp.float32) + dt_bias)
    log_heads = -(step_size * decay_rate)
    first_channel = blk_index * channels
    channel_head = (first_channel + jnp.arange(channels, dtype=jnp.int32)) // HEADDIM
    head_low = first_channel // HEADDIM
    head_high = (first_channel + channels - 1) // HEADDIM
    mask_high = (channel_head == head_high).astype(jnp.float32)
    mask_low = 1.0 - mask_high
    step_pair = jnp.concatenate(
        [
            lax.dynamic_slice_in_dim(step_size, head_low, 1, 1),
            lax.dynamic_slice_in_dim(step_size, head_high, 1, 1),
        ],
        axis=1,
    )
    log_pair = jnp.concatenate(
        [
            lax.dynamic_slice_in_dim(log_heads, head_low, 1, 1),
            lax.dynamic_slice_in_dim(log_heads, head_high, 1, 1),
        ],
        axis=1,
    )
    step_channel = step_pair[:, 0:1] * mask_low + step_pair[:, 1:2] * mask_high
    driven = conv_value * step_channel
    slot_masks = (mask_low, mask_high)
    blocks = tokens_all // SCAN_BLOCK
    order = jnp.arange(SCAN_BLOCK, dtype=jnp.int32)
    causal = order[:, None] >= order[None, :]

    def block_step(carry, inputs):
        carried, previous = carry
        drive_block, in_block, out_block, log_block, seg_block = inputs
        cumulative = jnp.dot(causal.astype(jnp.float32), log_block, precision=HIGH)
        gram = jnp.dot(out_block, in_block.T, precision=HIGH)
        same = (seg_block[:, None] == seg_block[None, :]) & causal
        result = jnp.zeros((SCAN_BLOCK, channels), jnp.float32)
        for slot_index in range(2):
            column = cumulative[:, slot_index]
            spread = jnp.minimum(column[:, None] - column[None, :], 0.0)
            weights = jnp.where(same, jnp.exp(spread), 0.0)
            result = result + jnp.dot(
                gram * weights, drive_block * slot_masks[slot_index], precision=HIGH
            )
        carried_in = carried * (seg_block[0] == previous).astype(jnp.float32)
        rising = jnp.exp(cumulative[:, 0:1]) * mask_low + jnp.exp(cumulative[:, 1:2]) * mask_high
        leading = (seg_block == seg_block[0]).astype(jnp.float32)[:, None]
        result = result + leading * rising * jnp.dot(out_block, carried_in.T, precision=HIGH)
        trailing = (seg_block == seg_block[-1]).astype(jnp.float32)[:, None]
        tail_low = jnp.exp(cumulative[-1:, 0:1] - cumulative[:, 0:1])
        tail_high = jnp.exp(cumulative[-1:, 1:2] - cumulative[:, 1:2])
        tail = tail_low * mask_low + tail_high * mask_high
        whole_block = (seg_block[-1] == seg_block[0]).astype(jnp.float32)
        carried_new = whole_block * rising[-1][:, None] * carried_in + jnp.dot(
            (drive_block * tail * trailing).T, in_block, precision=HIGH
        )
        return ((carried_new, seg_block[-1]), result)

    initial = (jnp.zeros((channels, NSTATE), jnp.float32), jnp.int32(-1))
    scan_inputs = (
        driven.reshape(blocks, SCAN_BLOCK, channels),
        input_map.reshape(blocks, SCAN_BLOCK, NSTATE),
        output_map.reshape(blocks, SCAN_BLOCK, NSTATE),
        log_pair.reshape(blocks, SCAN_BLOCK, 2),
        segment.reshape(blocks, SCAN_BLOCK),
    )
    final_carry, scanned = lax.scan(block_step, initial, scan_inputs)
    mixed = scanned.reshape(tokens_all, channels) + jnp.take(d_skip, channel_head) * conv_value
    gated = mixed * jax.nn.silu(gate_half)
    squares = lax.psum(jnp.sum(gated * gated, axis=1), "blk")
    inverse = lax.rsqrt(squares / inner_total + EPSILON)
    gated_norm = (gated * inverse[:, None] * norm_gain).astype(jnp.bfloat16)
    delta_own = lax.psum_scatter(
        jnp.dot(gated_norm, w_out, preferred_element_type=jnp.float32),
        "blk",
        scatter_dimension=0,
        tiled=True,
    )
    layer_own = (rows_own.astype(jnp.float32) + delta_own).astype(jnp.bfloat16)
    logits = jnp.dot(
        lax.all_gather(final_norm(layer_own, final_gain), "blk", axis=0, tiled=True),
        w_head,
        preferred_element_type=jnp.float32,
    )
    vocab_local = w_head.shape[1]
    local_label = labels[0] - blk_index * vocab_local
    hit = jnp.arange(vocab_local, dtype=jnp.int32)[None, :] == local_label[:, None]
    target_local = jnp.sum(jnp.where(hit, logits, 0.0), axis=1)
    top_local = jnp.max(logits, axis=1)
    top_all = lax.pmax(top_local, "blk")
    expsum_local = jnp.sum(jnp.exp(logits - top_all[:, None]), axis=1)
    expsum_all, target_all = lax.psum((expsum_local, target_local), "blk")
    logprob = target_all - (top_all + jnp.log(expsum_all))
    token_own = lax.dynamic_slice_in_dim(logprob, blk_index * rows_count, rows_count, 0)
    seqs_count = lengths.shape[1]
    onehot = (segment[:, None] == jnp.arange(seqs_count, dtype=jnp.int32)[None, :]).astype(
        jnp.float32
    )
    sums = jnp.dot(logprob, onehot, precision=HIGH)
    seq_index = lax.axis_index("seq")
    mine = lax.dynamic_slice_in_dim(owners, seq_index * seqs_count, seqs_count, 0)
    placement = (mine[:, None] == jnp.arange(owners.shape[0], dtype=jnp.int32)[None, :]).astype(
        jnp.float32
    )
    spread_sums = jnp.dot(sums, placement, precision=HIGH)
    seq_own = lax.psum_scatter(spread_sums, "seq", scatter_dimension=0, tiled=True)
    return (layer_own[None], token_own[None], seq_own)


LANES = 128
PLANES = 4
NT = (((1,), (1,)), ((), ()))
F32 = jnp.float32
BF16 = jnp.bfloat16


def iota(shape, dim):
    return lax.broadcasted_iota(jnp.int32, shape, dim)


def remote(source, target, send_sem, recv_sem, device):
    return pltpu.make_async_remote_copy(
        src_ref=source,
        dst_ref=target,
        send_sem=send_sem,
        recv_sem=recv_sem,
        device_id={"blk": device},
        device_id_type=pl.DeviceIdType.MESH,
    )


class Gather:
    def __init__(self, buf, z_sem, p_sem, c_sem, recv_sem, count, me):
        self.buf, self.z_sem, self.p_sem, self.c_sem, self.recv_sem = buf, z_sem, p_sem, c_sem, recv_sem
        self.me, self.planes, self.width = me, PLANES, count // (2 * PLANES)
        self.core = me % 2
        self.spot = (me // 2) % self.width
        self.plane = me // (2 * self.width)
        self.sibling = me + 1 - 2 * self.core

    def index(self, plane, spot, core):
        return (plane * self.width + spot) * 2 + core

    def copy(self, block, send_sem, device):
        return remote(self.buf.at[block], self.buf.at[block], send_sem, self.recv_sem.at[block], device)

    def plane_at(self, step):
        return (self.plane + step) % self.planes

    def spot_at(self, step):
        return (self.spot + step) % self.width

    def to_plane(self, block, step):
        def one(d, carry):
            device = self.index(self.plane, self.spot_at(d), self.core)
            self.copy(block, self.p_sem.at[step * (self.width - 1) + d - 1], device).start()
            return carry

        lax.fori_loop(1, self.width, one, 0)

    def to_core(self, block, slot):
        self.copy(block, self.c_sem.at[slot], self.sibling).start()

    def start(self):
        def one(d, carry):
            device = self.index(self.plane_at(d), self.spot, self.core)
            self.copy(self.me, self.z_sem.at[d - 1], device).start()
            return carry

        lax.fori_loop(1, self.planes, one, 0)
        self.to_plane(self.me, 0)
        self.to_core(self.me, 0)

    def arrived(self, block):
        self.copy(block, self.c_sem.at[0], self.sibling).wait_recv()

    def forward(self):
        def along(d, carry):
            block = self.index(self.plane_at(d), self.spot, self.core)
            self.arrived(block)
            self.to_plane(block, d)
            self.to_core(block, d)
            return carry

        lax.fori_loop(1, self.planes, along, 0)

        def within(i, carry):
            step, d = i // (self.width - 1), i % (self.width - 1) + 1
            block = self.index(self.plane_at(step), self.spot_at(d), self.core)
            self.arrived(block)
            self.to_core(block, self.planes + i)
            return carry

        lax.fori_loop(0, self.planes * (self.width - 1), within, 0)

    def finish(self):
        def last(i, carry):
            block = self.index(i // self.width, i % self.width, 1 - self.core)
            self.arrived(block)
            return carry

        lax.fori_loop(0, self.planes * self.width, last, 0)

    def drain(self):
        for sem, number in (
            (self.z_sem, self.planes - 1),
            (self.p_sem, self.planes * (self.width - 1)),
            (self.c_sem, self.planes * self.width),
        ):
            def one(i, carry, sem=sem):
                self.copy(self.me, sem.at[i], self.sibling).wait_send()
                return carry

            lax.fori_loop(0, number, one, 0)


def silu(x):
    return x * jax.nn.sigmoid(x)


def rolled_conv(values, taps, position):
    total = values * taps[0:1]
    for shift_by in range(1, CONV):
        moved = pltpu.roll(values, shift_by, 0)
        total = total + jnp.where(position >= shift_by, moved * taps[shift_by : shift_by + 1], 0.0)
    return total


def pick(row, index):
    lanes = iota(row.shape, 1)
    return jnp.sum(jnp.where(lanes == index, row, 0.0), axis=1, keepdims=True)


def column_of(row):
    size = row.shape[1]
    same = iota((size, size), 0) == iota((size, size), 1)
    return jnp.sum(jnp.where(same, row, 0.0), axis=1, keepdims=True)


def kernel(
    count,
    hidden,
    labels,
    lengths,
    owners,
    w_inner,
    w_bcdt,
    conv_inner,
    conv_bc,
    dt_bias,
    decay_rate,
    d_skip,
    norm_gain,
    w_out,
    final_gain,
    w_head,
    layer_out,
    token_out,
    seq_out,
    h_buf,
    g_buf,
    l_buf,
    w_src,
    w_dst,
    f_buf,
    wide,
    heads,
    tail,
    heads_t,
    scores,
    h_z, h_p, h_c, h_r,
    g_z, g_p, g_c, g_r,
    l_z, l_p, l_c, l_r,
    w_s, w_r,
    f_s, f_r,
    head_sem,
):
    me = lax.axis_index("blk")
    rows = hidden.shape[0]
    depth = hidden.shape[1]
    tokens = rows * count
    channels = w_inner.shape[1] // 2
    columns = depth // count
    vocab = w_head.shape[1]
    padded = heads_t.shape[0]

    fetch = pltpu.make_async_copy(w_head, heads, head_sem)
    fetch.start()
    h_buf[me] = hidden[...]

    barrier = pltpu.get_barrier_semaphore()

    def greet(d, carry):
        pl.semaphore_signal(
            barrier, inc=1, device_id={"blk": (me + d) % count}, device_id_type=pl.DeviceIdType.MESH
        )
        return carry

    lax.fori_loop(1, count, greet, 0)
    pl.semaphore_wait(barrier, count - 1)

    h_all = Gather(h_buf, h_z, h_p, h_c, h_r, count, me)
    h_all.start()

    wide[...] = w_out[...].astype(F32) * column_of(norm_gain[...])
    for e in range(count):
        w_src[e, :, 0:columns] = wide[:, e * columns : (e + 1) * columns].astype(BF16)
    h_all.forward()

    def give(d, carry):
        device = (me + d) % count
        remote(w_src.at[device], w_dst.at[me], w_s.at[d], w_r.at[d], device).start()
        return carry

    lax.fori_loop(1, count, give, 0)
    w_dst[me] = w_src[me]

    places = lengths.shape[1]
    length_row = lengths[...].astype(F32)
    length_col = column_of(length_row)
    later = iota((places, places), 0) < iota((places, places), 1)
    starts_row = jnp.sum(jnp.where(later, length_col, 0.0), axis=0, keepdims=True)
    starts_col = column_of(starts_row)
    token_row = iota((places, tokens), 1).astype(F32)
    begun = token_row >= starts_col
    start_row = jnp.max(jnp.where(begun, starts_col, 0.0), axis=0, keepdims=True)
    segment_row = jnp.sum(jnp.where(begun, 1.0, 0.0), axis=0, keepdims=True) - 1.0
    token_col = iota((tokens, places), 0).astype(F32)
    start_col = jnp.max(jnp.where(token_col >= starts_row, starts_row, 0.0), axis=1, keepdims=True)
    position = iota((tokens, 1), 0).astype(F32) - start_col

    h_all.finish()
    gathered = h_buf[...].reshape(tokens, depth)
    inner = jnp.dot(gathered, w_inner[...], preferred_element_type=F32).astype(BF16).astype(F32)
    state = jnp.dot(gathered, w_bcdt[...], preferred_element_type=F32).astype(BF16).astype(F32)
    gate = inner[:, :channels]
    conv_value = silu(rolled_conv(inner[:, channels:], conv_inner[...], position))
    conv_state = silu(rolled_conv(state[:, : 2 * NSTATE], conv_bc[...], position))
    raw = state[:, 2 * NSTATE :] + dt_bias[...]
    step_size = jnp.maximum(raw, 0.0) + jnp.log1p(jnp.exp(-jnp.abs(raw)))
    first = me * channels
    low = first // HEADDIM
    high = (first + channels - 1) // HEADDIM
    mask_high = (iota((1, channels), 1) + first >= high * HEADDIM).astype(F32)
    masks = (1.0 - mask_high, mask_high)
    steps = (pick(step_size, low), pick(step_size, high))
    rates = (pick(decay_rate[...], low), pick(decay_rate[...], high))
    skip = pick(d_skip[...], low) * masks[0] + pick(d_skip[...], high) * masks[1]
    driven = conv_value * (steps[0] * masks[0] + steps[1] * masks[1])
    lanes = iota((tokens, LANES), 1)
    logs = jnp.where(
        lanes == 0, -(steps[0] * rates[0]), jnp.where(lanes == 1, -(steps[1] * rates[1]), 0.0)
    )
    size = SCAN_BLOCK
    causal = iota((size, size), 0) >= iota((size, size), 1)
    lower = causal.astype(F32)
    blocks = tokens // size
    cuts = [slice(b * size, (b + 1) * size) for b in range(blocks)]
    sums_col = [jnp.dot(lower, logs[cut], precision=HIGH) for cut in cuts]
    sums_row = [jnp.transpose(s) for s in sums_col]
    results = []
    for b in range(blocks):
        result = jnp.zeros((size, channels), F32)
        for a in range(b + 1):
            gram = lax.dot_general(
                conv_state[cuts[b], NSTATE:], conv_state[cuts[a], :NSTATE], NT, precision=HIGH
            )
            same = start_col[cuts[b]] == start_row[:, cuts[a]]
            if a == b:
                same = same & causal
            for slot in range(2):
                rise = sums_col[b][:, slot : slot + 1]
                fall = sums_row[a][slot : slot + 1, :]
                if a == b:
                    spread = jnp.minimum(rise - fall, 0.0)
                else:
                    rest = sums_col[a][size - 1 : size, slot : slot + 1] - fall
                    for between in range(a + 1, b):
                        rest = rest + sums_col[between][size - 1 : size, slot : slot + 1]
                    spread = rise + jnp.minimum(rest, 0.0)
                weights = jnp.where(same, jnp.exp(spread), 0.0)
                result = result + jnp.dot(
                    gram * weights, driven[cuts[a]] * masks[slot], precision=HIGH
                )
        results.append(result)
    mixed = jnp.concatenate(results, axis=0) + skip * conv_value
    gated = (mixed * silu(gate)).astype(BF16)
    eye = (iota((channels, channels), 0) == iota((channels, channels), 1)).astype(BF16)
    g_buf[me] = lax.dot_general(eye, gated, NT, preferred_element_type=F32).astype(BF16)

    g_all = Gather(g_buf, g_z, g_p, g_c, g_r, count, me)
    g_all.start()
    own_columns = (iota((columns, depth), 1) == iota((columns, depth), 0) + me * columns).astype(BF16)
    hidden_t = lax.dot_general(own_columns, gathered, NT, preferred_element_type=F32)
    g_all.forward()
    fetch.wait()
    tail[...] = jnp.zeros_like(tail)
    for k in range(depth // LANES):
        span = slice(k * LANES, (k + 1) * LANES)
        gain = final_gain[:, span]
        for j in range(padded // LANES):
            if (j + 1) * LANES <= vocab:
                block = heads[span, j * LANES : (j + 1) * LANES].astype(F32)
            else:
                tail[:, : vocab - j * LANES] = heads[span, j * LANES : vocab].astype(F32)
                block = tail[...]
            heads_t[j * LANES : (j + 1) * LANES, span] = (jnp.transpose(block) * gain).astype(BF16)

    def taken(d, carry):
        device = (me + count - d) % count
        remote(w_src.at[device], w_dst.at[device], w_s.at[d], w_r.at[d], device).wait_recv()
        return carry

    lax.fori_loop(1, count, taken, 0)
    w_columns = w_dst[...].reshape(count * channels, LANES)[:, :columns]
    g_all.finish()
    g_t = g_buf[...].reshape(count * channels, tokens)
    wide_g = g_t.astype(F32)
    squares = jnp.sum(wide_g * wide_g, axis=0, keepdims=True)
    inverse = lax.rsqrt(squares / (count * channels) + EPSILON)
    delta = lax.dot_general(
        w_columns, g_t, (((0,), (0,)), ((), ())), preferred_element_type=F32
    )
    l_buf[me] = (hidden_t + delta * inverse).astype(BF16)

    l_all = Gather(l_buf, l_z, l_p, l_c, l_r, count, me)
    l_all.start()
    l_all.forward()
    l_all.finish()
    layer_t = l_buf[...].reshape(depth, tokens)
    own_rows = (iota((rows, tokens), 1) == iota((rows, tokens), 0) + me * rows).astype(BF16)
    layer_out[...] = lax.dot_general(own_rows, layer_t, NT, preferred_element_type=F32).astype(BF16)
    wide_l = layer_t.astype(F32)
    scale = lax.rsqrt(jnp.sum(wide_l * wide_l, axis=0, keepdims=True) / depth + EPSILON)
    label = labels[...] - me * vocab
    top = jnp.full((1, tokens), -jnp.inf, F32)
    target = jnp.zeros((1, tokens), F32)
    for j in range(padded // LANES):
        piece = jnp.dot(
            heads_t[j * LANES : (j + 1) * LANES, :], layer_t, preferred_element_type=F32
        ) * scale
        entry = iota((LANES, tokens), 0) + j * LANES
        target = target + jnp.sum(
            jnp.where(entry == jnp.where(label < vocab, label, -1), piece, 0.0), axis=0, keepdims=True
        )
        if (j + 1) * LANES > vocab:
            piece = jnp.where(entry < vocab, piece, -jnp.inf)
        scores[j * LANES : (j + 1) * LANES, :] = piece
        top = jnp.maximum(top, jnp.max(piece, axis=0, keepdims=True))
    total = jnp.sum(jnp.exp(scores[...] - top), axis=0, keepdims=True)
    local = top + jnp.log(total)
    parts = tokens // LANES
    for i in range(parts):
        f_buf[me, i : i + 1, :] = local[:, i * LANES : (i + 1) * LANES]
        f_buf[me, parts + i : parts + i + 1, :] = target[:, i * LANES : (i + 1) * LANES]

    def tell(d, carry):
        device = (me + d) % count
        remote(f_buf.at[me], f_buf.at[me], f_s.at[d], f_r.at[d], device).start()
        return carry

    lax.fori_loop(1, count, tell, 0)

    for gather in (h_all, g_all, l_all):
        gather.drain()

    def heard(d, carry):
        device = (me + count - d) % count
        remote(f_buf.at[device], f_buf.at[device], f_s.at[d], f_r.at[d], device).wait_recv()
        return carry

    lax.fori_loop(1, count, heard, 0)
    every = f_buf[...]
    ends = every[:, :parts, :]
    peak = jnp.max(ends, axis=0)
    norm = peak + jnp.log(jnp.sum(jnp.exp(ends - peak[None]), axis=0))
    square = jnp.sum(every[:, parts:, :], axis=0) - norm
    logprob = jnp.concatenate([square[i : i + 1, :] for i in range(parts)], axis=1)
    token_out[...] = lax.dot_general(
        jnp.broadcast_to(logprob, (8, tokens)), own_rows.astype(F32), NT, precision=HIGH
    )[0:1, :]
    member = iota((places, tokens), 0).astype(F32) == segment_row
    sums = jnp.sum(jnp.where(member, logprob, 0.0), axis=1, keepdims=True)
    owner_col = column_of(owners[...].astype(F32))
    slots = iota((places, places), 1).astype(F32) == owner_col
    seq_out[...] = jnp.sum(jnp.where(slots, sums, 0.0), axis=0, keepdims=True)

    def sent(d, carry):
        remote(w_src.at[me], w_dst.at[me], w_s.at[d], w_r.at[d], h_all.sibling).wait_send()
        remote(f_buf.at[me], f_buf.at[me], f_s.at[d], f_r.at[d], h_all.sibling).wait_send()
        return carry

    lax.fori_loop(1, count, sent, 0)


def fused(
    hidden,
    labels,
    lengths,
    owners,
    w_inner,
    w_bcdt,
    conv_inner,
    conv_bc,
    dt_bias,
    decay_rate,
    d_skip,
    norm_gain,
    w_out,
    final_gain,
    w_head,
):
    count = lax.axis_size("blk")
    rows, depth = hidden.shape[1:]
    tokens = rows * count
    channels = w_inner.shape[2]
    vocab = w_head.shape[1]
    padded = -(-vocab // LANES) * LANES
    width = count // (2 * PLANES)
    vmem = pl.BlockSpec(memory_space=pltpu.VMEM)
    gather_sems = [
        pltpu.SemaphoreType.DMA((PLANES - 1,)),
        pltpu.SemaphoreType.DMA((PLANES * (width - 1),)),
        pltpu.SemaphoreType.DMA((PLANES * width,)),
        pltpu.SemaphoreType.DMA((count,)),
    ]
    layer, token, seq = pl.pallas_call(
        functools.partial(kernel, count),
        out_shape=(
            jax.ShapeDtypeStruct((rows, depth), BF16),
            jax.ShapeDtypeStruct((1, rows), F32),
            jax.ShapeDtypeStruct((1, owners.shape[0]), F32),
        ),
        in_specs=[vmem] * 14 + [pl.BlockSpec(memory_space=pl.ANY)],
        out_specs=(vmem, vmem, vmem),
        scratch_shapes=[
            pltpu.VMEM((count, rows, depth), BF16),
            pltpu.VMEM((count, channels, tokens), BF16),
            pltpu.VMEM((count, depth // count, tokens), BF16),
            pltpu.VMEM((count, channels, LANES), BF16),
            pltpu.VMEM((count, channels, LANES), BF16),
            pltpu.VMEM((count, 2 * tokens // LANES, LANES), F32),
            pltpu.VMEM((channels, depth), F32),
            pltpu.VMEM((depth, vocab), BF16),
            pltpu.VMEM((LANES, LANES), F32),
            pltpu.VMEM((padded, depth), BF16),
            pltpu.VMEM((padded, tokens), F32),
        ]
        + gather_sems * 3
        + [pltpu.SemaphoreType.DMA((count,))] * 4
        + [pltpu.SemaphoreType.DMA],
        compiler_params=pltpu.CompilerParams(
            collective_id=0, has_side_effects=True, vmem_limit_bytes=56 * 1024 * 1024
        ),
    )(
        hidden[0],
        labels,
        lengths,
        owners.reshape(1, -1),
        w_inner.reshape(depth, 2 * channels),
        w_bcdt,
        conv_inner,
        conv_bc,
        dt_bias.reshape(1, -1),
        decay_rate.reshape(1, -1),
        d_skip.reshape(1, -1),
        norm_gain.reshape(1, -1),
        w_out,
        final_gain.reshape(1, -1),
        w_head,
    )
    return (layer[None], token, seq[0])


def layer(*args):
    hidden, w_inner = args[0], args[4]
    count = lax.axis_size("blk")
    rows, depth = hidden.shape[1:]
    tokens = rows * count
    whole = lax.axis_size("seq") == 1 and count % (4 * PLANES) == 0
    tiled = rows % 16 == 0 and w_inner.shape[2] % 16 == 0 and depth % (16 * count) == 0
    sized = depth // count <= LANES and tokens % SCAN_BLOCK == 0 and depth % LANES == 0
    return (fused if whole and tiled and sized else shards)(*args)


def solution(mesh):
    in_specs = (
        P(("mp", "seq"), "blk", None),
        P("seq", None),
        P("seq", None),
        P(),
        P("mp", None, "blk"),
        P("mp", None),
        P("mp", "blk"),
        P("mp", None),
        P("mp"),
        P("mp"),
        P("mp"),
        P(("mp", "blk")),
        P(("mp", "blk"), None),
        P("mp"),
        P("mp", "blk"),
    )
    out_specs = (P(("mp", "seq"), "blk", None), P(("mp", "seq"), "blk"), P(("mp", "seq")))
    return jax.shard_map(layer, mesh=mesh, in_specs=in_specs, out_specs=out_specs, check_vma=False)
```

```python
import functools

import jax
import jax.numpy as jnp
from jax import lax
from jax.experimental import pallas as pl
from jax.experimental.pallas import tpu as pltpu
from jax.sharding import PartitionSpec as P

D = 1536
HEADDIM = 64
NSTATE = 128
SCAN_BLOCK = 256
CONV = 4


EPSILON = 1e-05
HIGH = lax.Precision.HIGHEST


def segments_of(lengths, count):
    order = jnp.arange(lengths.shape[0], dtype=jnp.int32)
    earlier = order[None, :] < order[:, None]
    starts = jnp.sum(jnp.where(earlier, lengths[None, :], 0), axis=-1)
    places = jnp.arange(count, dtype=jnp.int32)
    segment = jnp.sum((places[:, None] >= starts[None, :]).astype(jnp.int32), axis=-1) - 1
    first = jnp.take(starts, segment)
    return (segment, places - first)


def causal_conv(values, weights, position):
    total = values * weights[0]
    for shift_by in range(1, CONV):
        moved = jnp.concatenate(
            [jnp.zeros_like(values[:shift_by, :]), values[:-shift_by, :]], axis=0
        )
        total = (
            total + moved * weights[shift_by] * (position >= shift_by).astype(jnp.float32)[:, None]
        )
    return total


def final_norm(values, gain):
    widened = values.astype(jnp.float32)
    scale = lax.rsqrt(jnp.mean(widened * widened, axis=-1, keepdims=True) + EPSILON)
    return (widened * scale * gain).astype(jnp.bfloat16)


def shards(
    hidden,
    labels,
    lengths,
    owners,
    w_inner,
    w_bcdt,
    conv_inner,
    conv_bc,
    dt_bias,
    decay_rate,
    d_skip,
    norm_gain,
    w_out,
    final_gain,
    w_head,
):
    rows_own = hidden[0]
    rows_count = rows_own.shape[0]
    blk_count = lax.axis_size("blk")
    blk_index = lax.axis_index("blk")
    gathered = lax.all_gather(rows_own, "blk", axis=0, tiled=True)
    tokens_all = gathered.shape[0]
    channels = w_inner.shape[2]
    inner_total = channels * blk_count
    inner_proj = jnp.dot(
        gathered, w_inner.reshape(D, 2 * channels), preferred_element_type=jnp.float32
    ).astype(jnp.bfloat16)
    state_proj = jnp.dot(gathered, w_bcdt, preferred_element_type=jnp.float32).astype(jnp.bfloat16)
    gate_half = inner_proj[:, :channels].astype(jnp.float32)
    segment, position = segments_of(lengths[0], tokens_all)
    conv_value = jax.nn.silu(
        causal_conv(inner_proj[:, channels:].astype(jnp.float32), conv_inner, position)
    )
    conv_state = jax.nn.silu(
        causal_conv(state_proj[:, : 2 * NSTATE].astype(jnp.float32), conv_bc, position)
    )
    input_map = conv_state[:, :NSTATE]
    output_map = conv_state[:, NSTATE:]
    step_size = jax.nn.softplus(state_proj[:, 2 * NSTATE :].astype(jnp.float32) + dt_bias)
    log_heads = -(step_size * decay_rate)
    first_channel = blk_index * channels
    channel_head = (first_channel + jnp.arange(channels, dtype=jnp.int32)) // HEADDIM
    head_low = first_channel // HEADDIM
    head_high = (first_channel + channels - 1) // HEADDIM
    mask_high = (channel_head == head_high).astype(jnp.float32)
    mask_low = 1.0 - mask_high
    step_pair = jnp.concatenate(
        [
            lax.dynamic_slice_in_dim(step_size, head_low, 1, 1),
            lax.dynamic_slice_in_dim(step_size, head_high, 1, 1),
        ],
        axis=1,
    )
    log_pair = jnp.concatenate(
        [
            lax.dynamic_slice_in_dim(log_heads, head_low, 1, 1),
            lax.dynamic_slice_in_dim(log_heads, head_high, 1, 1),
        ],
        axis=1,
    )
    step_channel = step_pair[:, 0:1] * mask_low + step_pair[:, 1:2] * mask_high
    driven = conv_value * step_channel
    slot_masks = (mask_low, mask_high)
    blocks = tokens_all // SCAN_BLOCK
    order = jnp.arange(SCAN_BLOCK, dtype=jnp.int32)
    causal = order[:, None] >= order[None, :]

    def block_step(carry, inputs):
        carried, previous = carry
        drive_block, in_block, out_block, log_block, seg_block = inputs
        cumulative = jnp.dot(causal.astype(jnp.float32), log_block, precision=HIGH)
        gram = jnp.dot(out_block, in_block.T, precision=HIGH)
        same = (seg_block[:, None] == seg_block[None, :]) & causal
        result = jnp.zeros((SCAN_BLOCK, channels), jnp.float32)
        for slot_index in range(2):
            column = cumulative[:, slot_index]
            spread = jnp.minimum(column[:, None] - column[None, :], 0.0)
            weights = jnp.where(same, jnp.exp(spread), 0.0)
            result = result + jnp.dot(
                gram * weights, drive_block * slot_masks[slot_index], precision=HIGH
            )
        carried_in = carried * (seg_block[0] == previous).astype(jnp.float32)
        rising = jnp.exp(cumulative[:, 0:1]) * mask_low + jnp.exp(cumulative[:, 1:2]) * mask_high
        leading = (seg_block == seg_block[0]).astype(jnp.float32)[:, None]
        result = result + leading * rising * jnp.dot(out_block, carried_in.T, precision=HIGH)
        trailing = (seg_block == seg_block[-1]).astype(jnp.float32)[:, None]
        tail_low = jnp.exp(cumulative[-1:, 0:1] - cumulative[:, 0:1])
        tail_high = jnp.exp(cumulative[-1:, 1:2] - cumulative[:, 1:2])
        tail = tail_low * mask_low + tail_high * mask_high
        whole_block = (seg_block[-1] == seg_block[0]).astype(jnp.float32)
        carried_new = whole_block * rising[-1][:, None] * carried_in + jnp.dot(
            (drive_block * tail * trailing).T, in_block, precision=HIGH
        )
        return ((carried_new, seg_block[-1]), result)

    initial = (jnp.zeros((channels, NSTATE), jnp.float32), jnp.int32(-1))
    scan_inputs = (
        driven.reshape(blocks, SCAN_BLOCK, channels),
        input_map.reshape(blocks, SCAN_BLOCK, NSTATE),
        output_map.reshape(blocks, SCAN_BLOCK, NSTATE),
        log_pair.reshape(blocks, SCAN_BLOCK, 2),
        segment.reshape(blocks, SCAN_BLOCK),
    )
    final_carry, scanned = lax.scan(block_step, initial, scan_inputs)
    mixed = scanned.reshape(tokens_all, channels) + jnp.take(d_skip, channel_head) * conv_value
    gated = mixed * jax.nn.silu(gate_half)
    squares = lax.psum(jnp.sum(gated * gated, axis=1), "blk")
    inverse = lax.rsqrt(squares / inner_total + EPSILON)
    gated_norm = (gated * inverse[:, None] * norm_gain).astype(jnp.bfloat16)
    delta_own = lax.psum_scatter(
        jnp.dot(gated_norm, w_out, preferred_element_type=jnp.float32),
        "blk",
        scatter_dimension=0,
        tiled=True,
    )
    layer_own = (rows_own.astype(jnp.float32) + delta_own).astype(jnp.bfloat16)
    logits = jnp.dot(
        lax.all_gather(final_norm(layer_own, final_gain), "blk", axis=0, tiled=True),
        w_head,
        preferred_element_type=jnp.float32,
    )
    vocab_local = w_head.shape[1]
    local_label = labels[0] - blk_index * vocab_local
    hit = jnp.arange(vocab_local, dtype=jnp.int32)[None, :] == local_label[:, None]
    target_local = jnp.sum(jnp.where(hit, logits, 0.0), axis=1)
    top_local = jnp.max(logits, axis=1)
    top_all = lax.pmax(top_local, "blk")
    expsum_local = jnp.sum(jnp.exp(logits - top_all[:, None]), axis=1)
    expsum_all, target_all = lax.psum((expsum_local, target_local), "blk")
    logprob = target_all - (top_all + jnp.log(expsum_all))
    token_own = lax.dynamic_slice_in_dim(logprob, blk_index * rows_count, rows_count, 0)
    seqs_count = lengths.shape[1]
    onehot = (segment[:, None] == jnp.arange(seqs_count, dtype=jnp.int32)[None, :]).astype(
        jnp.float32
    )
    sums = jnp.dot(logprob, onehot, precision=HIGH)
    seq_index = lax.axis_index("seq")
    mine = lax.dynamic_slice_in_dim(owners, seq_index * seqs_count, seqs_count, 0)
    placement = (mine[:, None] == jnp.arange(owners.shape[0], dtype=jnp.int32)[None, :]).astype(
        jnp.float32
    )
    spread_sums = jnp.dot(sums, placement, precision=HIGH)
    seq_own = lax.psum_scatter(spread_sums, "seq", scatter_dimension=0, tiled=True)
    return (layer_own[None], token_own[None], seq_own)


LANES = 128
PLANES = 4
NT = (((1,), (1,)), ((), ()))
F32 = jnp.float32
BF16 = jnp.bfloat16


def iota(shape, dim):
    return lax.broadcasted_iota(jnp.int32, shape, dim)


def remote(source, target, send_sem, recv_sem, device):
    return pltpu.make_async_remote_copy(
        src_ref=source,
        dst_ref=target,
        send_sem=send_sem,
        recv_sem=recv_sem,
        device_id={"blk": device},
        device_id_type=pl.DeviceIdType.MESH,
    )


class Gather:
    def __init__(self, buf, z_sem, p_sem, c_sem, recv_sem, count, me):
        self.buf, self.z_sem, self.p_sem, self.c_sem, self.recv_sem = buf, z_sem, p_sem, c_sem, recv_sem
        self.me, self.planes, self.width = me, PLANES, count // (2 * PLANES)
        self.core = me % 2
        self.spot = (me // 2) % self.width
        self.plane = me // (2 * self.width)
        self.sibling = me + 1 - 2 * self.core

    def index(self, plane, spot, core):
        return (plane * self.width + spot) * 2 + core

    def copy(self, block, send_sem, device):
        return remote(self.buf.at[block], self.buf.at[block], send_sem, self.recv_sem.at[block], device)

    def plane_at(self, step):
        return (self.plane + step) % self.planes

    def spot_at(self, step):
        return (self.spot + step) % self.width

    def to_plane(self, block, step):
        def one(d, carry):
            device = self.index(self.plane, self.spot_at(d), self.core)
            self.copy(block, self.p_sem.at[step * (self.width - 1) + d - 1], device).start()
            return carry

        lax.fori_loop(1, self.width, one, 0)

    def to_core(self, block, slot):
        self.copy(block, self.c_sem.at[slot], self.sibling).start()

    def start(self):
        def one(d, carry):
            device = self.index(self.plane_at(d), self.spot, self.core)
            self.copy(self.me, self.z_sem.at[d - 1], device).start()
            return carry

        lax.fori_loop(1, self.planes, one, 0)
        self.to_plane(self.me, 0)
        self.to_core(self.me, 0)

    def arrived(self, block):
        self.copy(block, self.c_sem.at[0], self.sibling).wait_recv()

    def forward(self):
        def along(d, carry):
            block = self.index(self.plane_at(d), self.spot, self.core)
            self.arrived(block)
            self.to_plane(block, d)
            self.to_core(block, d)
            return carry

        lax.fori_loop(1, self.planes, along, 0)

        def within(i, carry):
            step, d = i // (self.width - 1), i % (self.width - 1) + 1
            block = self.index(self.plane_at(step), self.spot_at(d), self.core)
            self.arrived(block)
            self.to_core(block, self.planes + i)
            return carry

        lax.fori_loop(0, self.planes * (self.width - 1), within, 0)

    def finish(self):
        def last(i, carry):
            block = self.index(i // self.width, i % self.width, 1 - self.core)
            self.arrived(block)
            return carry

        lax.fori_loop(0, self.planes * self.width, last, 0)

    def drain(self):
        for sem, number in (
            (self.z_sem, self.planes - 1),
            (self.p_sem, self.planes * (self.width - 1)),
            (self.c_sem, self.planes * self.width),
        ):
            def one(i, carry, sem=sem):
                self.copy(self.me, sem.at[i], self.sibling).wait_send()
                return carry

            lax.fori_loop(0, number, one, 0)


def silu(x):
    return x * jax.nn.sigmoid(x)


def rolled_conv(values, taps, position):
    total = values * taps[0:1]
    for shift_by in range(1, CONV):
        moved = pltpu.roll(values, shift_by, 0)
        total = total + jnp.where(position >= shift_by, moved * taps[shift_by : shift_by + 1], 0.0)
    return total


def pick(row, index):
    lanes = iota(row.shape, 1)
    return jnp.sum(jnp.where(lanes == index, row, 0.0), axis=1, keepdims=True)


def split(values, number):
    parts = []
    for _ in range(number):
        part = values.astype(BF16)
        parts.append(part)
        values = values - part.astype(F32)
    return parts


def column_of(row):
    size = row.shape[1]
    same = iota((size, size), 0) == iota((size, size), 1)
    return jnp.sum(jnp.where(same, row, 0.0), axis=1, keepdims=True)


def kernel(
    count,
    hidden,
    labels,
    lengths,
    owners,
    w_inner,
    w_bcdt,
    conv_inner,
    conv_bc,
    dt_bias,
    decay_rate,
    d_skip,
    norm_gain,
    w_out,
    final_gain,
    w_head,
    layer_out,
    token_out,
    seq_out,
    h_buf,
    g_buf,
    l_buf,
    w_src,
    w_dst,
    f_buf,
    wide,
    heads,
    heads_t,
    scores,
    h_z, h_p, h_c, h_r,
    g_z, g_p, g_c, g_r,
    l_z, l_p, l_c, l_r,
    w_s, w_r,
    f_s, f_r,
    head_sem,
):
    me = lax.axis_index("blk")
    rows = hidden.shape[0]
    depth = hidden.shape[1]
    tokens = rows * count
    channels = w_inner.shape[0] // 2
    columns = depth // count
    vocab = w_head.shape[0]
    padded = heads_t.shape[0]

    fetch = pltpu.make_async_copy(w_head, heads, head_sem)
    fetch.start()
    h_buf[me] = hidden[...]

    barrier = pltpu.get_barrier_semaphore()

    def greet(d, carry):
        pl.semaphore_signal(
            barrier, inc=1, device_id={"blk": (me + d) % count}, device_id_type=pl.DeviceIdType.MESH
        )
        return carry

    lax.fori_loop(1, count, greet, 0)
    pl.semaphore_wait(barrier, count - 1)

    h_all = Gather(h_buf, h_z, h_p, h_c, h_r, count, me)
    h_all.start()

    wide[...] = w_out[...].astype(F32) * column_of(norm_gain[...])
    for e in range(count):
        w_src[e, :, 0:columns] = wide[:, e * columns : (e + 1) * columns].astype(BF16)
    h_all.forward()

    def give(d, carry):
        device = (me + d) % count
        remote(w_src.at[device], w_dst.at[me], w_s.at[d], w_r.at[d], device).start()
        return carry

    lax.fori_loop(1, count, give, 0)
    w_dst[me] = w_src[me]

    places = lengths.shape[1]
    length_row = lengths[...].astype(F32)
    length_col = column_of(length_row)
    later = iota((places, places), 0) < iota((places, places), 1)
    starts_row = jnp.sum(jnp.where(later, length_col, 0.0), axis=0, keepdims=True)
    starts_col = column_of(starts_row)
    token_row = iota((places, tokens), 1).astype(F32)
    begun = token_row >= starts_col
    start_row = jnp.max(jnp.where(begun, starts_col, 0.0), axis=0, keepdims=True)
    segment_row = jnp.sum(jnp.where(begun, 1.0, 0.0), axis=0, keepdims=True) - 1.0
    token_col = iota((tokens, places), 0).astype(F32)
    start_col = jnp.max(jnp.where(token_col >= starts_row, starts_row, 0.0), axis=1, keepdims=True)
    position = iota((tokens, 1), 0).astype(F32) - start_col

    h_all.finish()
    gathered = h_buf[...].reshape(tokens, depth)
    inner = lax.dot_general(gathered, w_inner[...], NT, preferred_element_type=F32)
    inner = inner.astype(BF16).astype(F32)
    state = lax.dot_general(gathered, w_bcdt[...], NT, preferred_element_type=F32)
    state = state.astype(BF16).astype(F32)
    gate = inner[:, :channels]
    conv_value = silu(rolled_conv(inner[:, channels:], conv_inner[...], position))
    conv_state = silu(rolled_conv(state[:, : 2 * NSTATE], conv_bc[...], position))
    raw = state[:, 2 * NSTATE :] + dt_bias[...]
    step_size = jnp.maximum(raw, 0.0) + jnp.log1p(jnp.exp(-jnp.abs(raw)))
    first = me * channels
    low = first // HEADDIM
    high = (first + channels - 1) // HEADDIM
    mask_high = (iota((1, channels), 1) + first >= high * HEADDIM).astype(F32)
    masks = (1.0 - mask_high, mask_high)
    steps = (pick(step_size, low), pick(step_size, high))
    rates = (pick(decay_rate[...], low), pick(decay_rate[...], high))
    skip = pick(d_skip[...], low) * masks[0] + pick(d_skip[...], high) * masks[1]
    driven = conv_value * (steps[0] * masks[0] + steps[1] * masks[1])
    lanes = iota((tokens, LANES), 1)
    logs = jnp.where(
        lanes == 0, -(steps[0] * rates[0]), jnp.where(lanes == 1, -(steps[1] * rates[1]), 0.0)
    )
    size = SCAN_BLOCK
    causal = iota((size, size), 0) >= iota((size, size), 1)
    lower = causal.astype(BF16)
    in_parts = split(conv_state[:, :NSTATE], 2)
    out_parts = split(conv_state[:, NSTATE:], 2)
    drive_parts = split(driven, 2)
    blocks = tokens // size
    cuts = [slice(b * size, (b + 1) * size) for b in range(blocks)]
    log_parts = split(logs, 3)
    sums_col = [
        sum(jnp.dot(lower, part[cut], preferred_element_type=F32) for part in log_parts)
        for cut in cuts
    ]
    sums_row = [jnp.transpose(s) for s in sums_col]
    results = []
    for b in range(blocks):
        result = jnp.zeros((size, channels), F32)
        for a in range(b + 1):
            gram = sum(
                lax.dot_general(
                    out_parts[i][cuts[b]], in_parts[j][cuts[a]], NT, preferred_element_type=F32
                )
                for i, j in ((0, 1), (1, 0), (0, 0))
            )
            same = start_col[cuts[b]] == start_row[:, cuts[a]]
            if a == b:
                same = same & causal
            for slot in range(2):
                rise = sums_col[b][:, slot : slot + 1]
                fall = sums_row[a][slot : slot + 1, :]
                if a == b:
                    spread = jnp.minimum(rise - fall, 0.0)
                else:
                    rest = sums_col[a][size - 1 : size, slot : slot + 1] - fall
                    for between in range(a + 1, b):
                        rest = rest + sums_col[between][size - 1 : size, slot : slot + 1]
                    spread = rise + jnp.minimum(rest, 0.0)
                weights = jnp.where(same, jnp.exp(spread), 0.0)
                mix_parts = split(gram * weights, 2)
                share = sum(
                    jnp.dot(mix_parts[i], drive_parts[j][cuts[a]], preferred_element_type=F32)
                    for i, j in ((0, 1), (1, 0), (0, 0))
                )
                result = result + share * masks[slot]
        results.append(result)
    mixed = jnp.concatenate(results, axis=0) + skip * conv_value
    gated = (mixed * silu(gate)).astype(BF16)
    eye = (iota((channels, channels), 0) == iota((channels, channels), 1)).astype(BF16)
    g_buf[me] = lax.dot_general(eye, gated, NT, preferred_element_type=F32).astype(BF16)

    g_all = Gather(g_buf, g_z, g_p, g_c, g_r, count, me)
    g_all.start()
    own_columns = (iota((columns, depth), 1) == iota((columns, depth), 0) + me * columns).astype(BF16)
    hidden_t = lax.dot_general(own_columns, gathered, NT, preferred_element_type=F32)
    g_all.forward()
    fetch.wait()
    heads_t[padded - LANES :, :] = jnp.zeros((LANES, depth), BF16)
    for k in range(depth // LANES):
        span = slice(k * LANES, (k + 1) * LANES)
        gain = final_gain[k : k + 1, :]
        heads_t[0:vocab, span] = (heads[:, span].astype(F32) * gain).astype(BF16)

    def taken(d, carry):
        device = (me + count - d) % count
        remote(w_src.at[device], w_dst.at[device], w_s.at[d], w_r.at[d], device).wait_recv()
        return carry

    lax.fori_loop(1, count, taken, 0)
    w_columns = w_dst[...].reshape(count * channels, LANES)[:, :columns]
    g_all.finish()
    g_t = g_buf[...].reshape(count * channels, tokens)
    wide_g = g_t.astype(F32)
    squares = jnp.sum(wide_g * wide_g, axis=0, keepdims=True)
    inverse = lax.rsqrt(squares / (count * channels) + EPSILON)
    delta = lax.dot_general(
        w_columns, g_t, (((0,), (0,)), ((), ())), preferred_element_type=F32
    )
    l_buf[me] = (hidden_t + delta * inverse).astype(BF16)

    l_all = Gather(l_buf, l_z, l_p, l_c, l_r, count, me)
    l_all.start()
    l_all.forward()
    l_all.finish()
    layer_t = l_buf[...].reshape(depth, tokens)
    own_rows = (iota((rows, tokens), 1) == iota((rows, tokens), 0) + me * rows).astype(BF16)
    layer_out[...] = lax.dot_general(own_rows, layer_t, NT, preferred_element_type=F32).astype(BF16)
    wide_l = layer_t.astype(F32)
    scale = lax.rsqrt(jnp.sum(wide_l * wide_l, axis=0, keepdims=True) / depth + EPSILON)
    label = labels[...] - me * vocab
    top = jnp.full((1, tokens), -jnp.inf, F32)
    target = jnp.zeros((1, tokens), F32)
    for j in range(padded // LANES):
        piece = jnp.dot(
            heads_t[j * LANES : (j + 1) * LANES, :], layer_t, preferred_element_type=F32
        ) * scale
        entry = iota((LANES, tokens), 0) + j * LANES
        target = target + jnp.sum(
            jnp.where(entry == jnp.where(label < vocab, label, -1), piece, 0.0), axis=0, keepdims=True
        )
        if (j + 1) * LANES > vocab:
            piece = jnp.where(entry < vocab, piece, -jnp.inf)
        scores[j * LANES : (j + 1) * LANES, :] = piece
        top = jnp.maximum(top, jnp.max(piece, axis=0, keepdims=True))
    total = jnp.sum(jnp.exp(scores[...] - top), axis=0, keepdims=True)
    local = top + jnp.log(total)
    parts = tokens // LANES
    for i in range(parts):
        f_buf[me, i : i + 1, :] = local[:, i * LANES : (i + 1) * LANES]
        f_buf[me, parts + i : parts + i + 1, :] = target[:, i * LANES : (i + 1) * LANES]

    def tell(d, carry):
        device = (me + d) % count
        remote(f_buf.at[me], f_buf.at[me], f_s.at[d], f_r.at[d], device).start()
        return carry

    lax.fori_loop(1, count, tell, 0)

    for gather in (h_all, g_all, l_all):
        gather.drain()

    def heard(d, carry):
        device = (me + count - d) % count
        remote(f_buf.at[device], f_buf.at[device], f_s.at[d], f_r.at[d], device).wait_recv()
        return carry

    lax.fori_loop(1, count, heard, 0)
    every = f_buf[...]
    ends = every[:, :parts, :]
    peak = jnp.max(ends, axis=0)
    norm = peak + jnp.log(jnp.sum(jnp.exp(ends - peak[None]), axis=0))
    square = jnp.sum(every[:, parts:, :], axis=0) - norm
    logprob = jnp.concatenate([square[i : i + 1, :] for i in range(parts)], axis=1)
    token_out[...] = lax.dot_general(
        jnp.broadcast_to(logprob, (8, tokens)), own_rows.astype(F32), NT, precision=HIGH
    )[0:1, :]
    member = iota((places, tokens), 0).astype(F32) == segment_row
    sums = jnp.sum(jnp.where(member, logprob, 0.0), axis=1, keepdims=True)
    owner_col = column_of(owners[...].astype(F32))
    slots = iota((places, places), 1).astype(F32) == owner_col
    seq_out[...] = jnp.sum(jnp.where(slots, sums, 0.0), axis=0, keepdims=True)

    def sent(d, carry):
        remote(w_src.at[me], w_dst.at[me], w_s.at[d], w_r.at[d], h_all.sibling).wait_send()
        remote(f_buf.at[me], f_buf.at[me], f_s.at[d], f_r.at[d], h_all.sibling).wait_send()
        return carry

    lax.fori_loop(1, count, sent, 0)


def fused(
    hidden,
    labels,
    lengths,
    owners,
    w_inner,
    w_bcdt,
    conv_inner,
    conv_bc,
    dt_bias,
    decay_rate,
    d_skip,
    norm_gain,
    w_out,
    final_gain,
    w_head,
):
    count = lax.axis_size("blk")
    rows, depth = hidden.shape[1:]
    tokens = rows * count
    channels = w_inner.shape[2]
    vocab = w_head.shape[1]
    padded = -(-vocab // LANES) * LANES
    width = count // (2 * PLANES)
    vmem = pl.BlockSpec(memory_space=pltpu.VMEM)
    gather_sems = [
        pltpu.SemaphoreType.DMA((PLANES - 1,)),
        pltpu.SemaphoreType.DMA((PLANES * (width - 1),)),
        pltpu.SemaphoreType.DMA((PLANES * width,)),
        pltpu.SemaphoreType.DMA((count,)),
    ]
    layer, token, seq = pl.pallas_call(
        functools.partial(kernel, count),
        out_shape=(
            jax.ShapeDtypeStruct((rows, depth), BF16),
            jax.ShapeDtypeStruct((1, rows), F32),
            jax.ShapeDtypeStruct((1, owners.shape[0]), F32),
        ),
        in_specs=[vmem] * 14 + [pl.BlockSpec(memory_space=pl.ANY)],
        out_specs=(vmem, vmem, vmem),
        scratch_shapes=[
            pltpu.VMEM((count, rows, depth), BF16),
            pltpu.VMEM((count, channels, tokens), BF16),
            pltpu.VMEM((count, depth // count, tokens), BF16),
            pltpu.VMEM((count, channels, LANES), BF16),
            pltpu.VMEM((count, channels, LANES), BF16),
            pltpu.VMEM((count, 2 * tokens // LANES, LANES), F32),
            pltpu.VMEM((channels, depth), F32),
            pltpu.VMEM((vocab, depth), BF16),
            pltpu.VMEM((padded, depth), BF16),
            pltpu.VMEM((padded, tokens), F32),
        ]
        + gather_sems * 3
        + [pltpu.SemaphoreType.DMA((count,))] * 4
        + [pltpu.SemaphoreType.DMA],
        compiler_params=pltpu.CompilerParams(
            collective_id=0, has_side_effects=True, vmem_limit_bytes=56 * 1024 * 1024
        ),
    )(
        hidden[0],
        labels,
        lengths,
        owners.reshape(1, -1),
        w_inner.transpose(1, 2, 0).reshape(2 * channels, depth),
        w_bcdt.T,
        conv_inner,
        conv_bc,
        dt_bias.reshape(1, -1),
        decay_rate.reshape(1, -1),
        d_skip.reshape(1, -1),
        norm_gain.reshape(1, -1),
        w_out,
        final_gain.reshape(-1, LANES),
        w_head.T,
    )
    return (layer[None], token, seq[0])


def layer(*args):
    hidden, w_inner = args[0], args[4]
    count = lax.axis_size("blk")
    rows, depth = hidden.shape[1:]
    tokens = rows * count
    whole = lax.axis_size("seq") == 1 and count % (4 * PLANES) == 0
    tiled = rows % 16 == 0 and w_inner.shape[2] % 16 == 0 and depth % (16 * count) == 0
    sized = depth // count <= LANES and tokens % SCAN_BLOCK == 0 and depth % LANES == 0
    return (fused if whole and tiled and sized else shards)(*args)


def solution(mesh):
    in_specs = (
        P(("mp", "seq"), "blk", None),
        P("seq", None),
        P("seq", None),
        P(),
        P("mp", None, "blk"),
        P("mp", None),
        P("mp", "blk"),
        P("mp", None),
        P("mp"),
        P("mp"),
        P("mp"),
        P(("mp", "blk")),
        P(("mp", "blk"), None),
        P("mp"),
        P("mp", "blk"),
    )
    out_specs = (P(("mp", "seq"), "blk", None), P(("mp", "seq"), "blk"), P(("mp", "seq")))
    return jax.shard_map(layer, mesh=mesh, in_specs=in_specs, out_specs=out_specs, check_vma=False)
```

```python
import functools

import jax
import jax.numpy as jnp
from jax import lax
from jax.experimental import pallas as pl
from jax.experimental.pallas import tpu as pltpu
from jax.sharding import PartitionSpec as P

D = 1536
HEADDIM = 64
NSTATE = 128
SCAN_BLOCK = 256
CONV = 4


EPSILON = 1e-05
HIGH = lax.Precision.HIGHEST


def segments_of(lengths, count):
    order = jnp.arange(lengths.shape[0], dtype=jnp.int32)
    earlier = order[None, :] < order[:, None]
    starts = jnp.sum(jnp.where(earlier, lengths[None, :], 0), axis=-1)
    places = jnp.arange(count, dtype=jnp.int32)
    segment = jnp.sum((places[:, None] >= starts[None, :]).astype(jnp.int32), axis=-1) - 1
    first = jnp.take(starts, segment)
    return (segment, places - first)


def causal_conv(values, weights, position):
    total = values * weights[0]
    for shift_by in range(1, CONV):
        moved = jnp.concatenate(
            [jnp.zeros_like(values[:shift_by, :]), values[:-shift_by, :]], axis=0
        )
        total = (
            total + moved * weights[shift_by] * (position >= shift_by).astype(jnp.float32)[:, None]
        )
    return total


def final_norm(values, gain):
    widened = values.astype(jnp.float32)
    scale = lax.rsqrt(jnp.mean(widened * widened, axis=-1, keepdims=True) + EPSILON)
    return (widened * scale * gain).astype(jnp.bfloat16)


def shards(
    hidden,
    labels,
    lengths,
    owners,
    w_inner,
    w_bcdt,
    conv_inner,
    conv_bc,
    dt_bias,
    decay_rate,
    d_skip,
    norm_gain,
    w_out,
    final_gain,
    w_head,
):
    rows_own = hidden[0]
    rows_count = rows_own.shape[0]
    blk_count = lax.axis_size("blk")
    blk_index = lax.axis_index("blk")
    gathered = lax.all_gather(rows_own, "blk", axis=0, tiled=True)
    tokens_all = gathered.shape[0]
    channels = w_inner.shape[2]
    inner_total = channels * blk_count
    inner_proj = jnp.dot(
        gathered, w_inner.reshape(D, 2 * channels), preferred_element_type=jnp.float32
    ).astype(jnp.bfloat16)
    state_proj = jnp.dot(gathered, w_bcdt, preferred_element_type=jnp.float32).astype(jnp.bfloat16)
    gate_half = inner_proj[:, :channels].astype(jnp.float32)
    segment, position = segments_of(lengths[0], tokens_all)
    conv_value = jax.nn.silu(
        causal_conv(inner_proj[:, channels:].astype(jnp.float32), conv_inner, position)
    )
    conv_state = jax.nn.silu(
        causal_conv(state_proj[:, : 2 * NSTATE].astype(jnp.float32), conv_bc, position)
    )
    input_map = conv_state[:, :NSTATE]
    output_map = conv_state[:, NSTATE:]
    step_size = jax.nn.softplus(state_proj[:, 2 * NSTATE :].astype(jnp.float32) + dt_bias)
    log_heads = -(step_size * decay_rate)
    first_channel = blk_index * channels
    channel_head = (first_channel + jnp.arange(channels, dtype=jnp.int32)) // HEADDIM
    head_low = first_channel // HEADDIM
    head_high = (first_channel + channels - 1) // HEADDIM
    mask_high = (channel_head == head_high).astype(jnp.float32)
    mask_low = 1.0 - mask_high
    step_pair = jnp.concatenate(
        [
            lax.dynamic_slice_in_dim(step_size, head_low, 1, 1),
            lax.dynamic_slice_in_dim(step_size, head_high, 1, 1),
        ],
        axis=1,
    )
    log_pair = jnp.concatenate(
        [
            lax.dynamic_slice_in_dim(log_heads, head_low, 1, 1),
            lax.dynamic_slice_in_dim(log_heads, head_high, 1, 1),
        ],
        axis=1,
    )
    step_channel = step_pair[:, 0:1] * mask_low + step_pair[:, 1:2] * mask_high
    driven = conv_value * step_channel
    slot_masks = (mask_low, mask_high)
    blocks = tokens_all // SCAN_BLOCK
    order = jnp.arange(SCAN_BLOCK, dtype=jnp.int32)
    causal = order[:, None] >= order[None, :]

    def block_step(carry, inputs):
        carried, previous = carry
        drive_block, in_block, out_block, log_block, seg_block = inputs
        cumulative = jnp.dot(causal.astype(jnp.float32), log_block, precision=HIGH)
        gram = jnp.dot(out_block, in_block.T, precision=HIGH)
        same = (seg_block[:, None] == seg_block[None, :]) & causal
        result = jnp.zeros((SCAN_BLOCK, channels), jnp.float32)
        for slot_index in range(2):
            column = cumulative[:, slot_index]
            spread = jnp.minimum(column[:, None] - column[None, :], 0.0)
            weights = jnp.where(same, jnp.exp(spread), 0.0)
            result = result + jnp.dot(
                gram * weights, drive_block * slot_masks[slot_index], precision=HIGH
            )
        carried_in = carried * (seg_block[0] == previous).astype(jnp.float32)
        rising = jnp.exp(cumulative[:, 0:1]) * mask_low + jnp.exp(cumulative[:, 1:2]) * mask_high
        leading = (seg_block == seg_block[0]).astype(jnp.float32)[:, None]
        result = result + leading * rising * jnp.dot(out_block, carried_in.T, precision=HIGH)
        trailing = (seg_block == seg_block[-1]).astype(jnp.float32)[:, None]
        tail_low = jnp.exp(cumulative[-1:, 0:1] - cumulative[:, 0:1])
        tail_high = jnp.exp(cumulative[-1:, 1:2] - cumulative[:, 1:2])
        tail = tail_low * mask_low + tail_high * mask_high
        whole_block = (seg_block[-1] == seg_block[0]).astype(jnp.float32)
        carried_new = whole_block * rising[-1][:, None] * carried_in + jnp.dot(
            (drive_block * tail * trailing).T, in_block, precision=HIGH
        )
        return ((carried_new, seg_block[-1]), result)

    initial = (jnp.zeros((channels, NSTATE), jnp.float32), jnp.int32(-1))
    scan_inputs = (
        driven.reshape(blocks, SCAN_BLOCK, channels),
        input_map.reshape(blocks, SCAN_BLOCK, NSTATE),
        output_map.reshape(blocks, SCAN_BLOCK, NSTATE),
        log_pair.reshape(blocks, SCAN_BLOCK, 2),
        segment.reshape(blocks, SCAN_BLOCK),
    )
    final_carry, scanned = lax.scan(block_step, initial, scan_inputs)
    mixed = scanned.reshape(tokens_all, channels) + jnp.take(d_skip, channel_head) * conv_value
    gated = mixed * jax.nn.silu(gate_half)
    squares = lax.psum(jnp.sum(gated * gated, axis=1), "blk")
    inverse = lax.rsqrt(squares / inner_total + EPSILON)
    gated_norm = (gated * inverse[:, None] * norm_gain).astype(jnp.bfloat16)
    delta_own = lax.psum_scatter(
        jnp.dot(gated_norm, w_out, preferred_element_type=jnp.float32),
        "blk",
        scatter_dimension=0,
        tiled=True,
    )
    layer_own = (rows_own.astype(jnp.float32) + delta_own).astype(jnp.bfloat16)
    logits = jnp.dot(
        lax.all_gather(final_norm(layer_own, final_gain), "blk", axis=0, tiled=True),
        w_head,
        preferred_element_type=jnp.float32,
    )
    vocab_local = w_head.shape[1]
    local_label = labels[0] - blk_index * vocab_local
    hit = jnp.arange(vocab_local, dtype=jnp.int32)[None, :] == local_label[:, None]
    target_local = jnp.sum(jnp.where(hit, logits, 0.0), axis=1)
    top_local = jnp.max(logits, axis=1)
    top_all = lax.pmax(top_local, "blk")
    expsum_local = jnp.sum(jnp.exp(logits - top_all[:, None]), axis=1)
    expsum_all, target_all = lax.psum((expsum_local, target_local), "blk")
    logprob = target_all - (top_all + jnp.log(expsum_all))
    token_own = lax.dynamic_slice_in_dim(logprob, blk_index * rows_count, rows_count, 0)
    seqs_count = lengths.shape[1]
    onehot = (segment[:, None] == jnp.arange(seqs_count, dtype=jnp.int32)[None, :]).astype(
        jnp.float32
    )
    sums = jnp.dot(logprob, onehot, precision=HIGH)
    seq_index = lax.axis_index("seq")
    mine = lax.dynamic_slice_in_dim(owners, seq_index * seqs_count, seqs_count, 0)
    placement = (mine[:, None] == jnp.arange(owners.shape[0], dtype=jnp.int32)[None, :]).astype(
        jnp.float32
    )
    spread_sums = jnp.dot(sums, placement, precision=HIGH)
    seq_own = lax.psum_scatter(spread_sums, "seq", scatter_dimension=0, tiled=True)
    return (layer_own[None], token_own[None], seq_own)


LANES = 128
PLANES = 4
NT = (((1,), (1,)), ((), ()))
F32 = jnp.float32
BF16 = jnp.bfloat16


def iota(shape, dim):
    return lax.broadcasted_iota(jnp.int32, shape, dim)


def remote(source, target, send_sem, recv_sem, device):
    return pltpu.make_async_remote_copy(
        src_ref=source,
        dst_ref=target,
        send_sem=send_sem,
        recv_sem=recv_sem,
        device_id={"blk": device},
        device_id_type=pl.DeviceIdType.MESH,
    )


class Gather:
    def __init__(self, buf, z_sem, p_sem, c_sem, recv_sem, count, me):
        self.buf, self.z_sem, self.p_sem, self.c_sem, self.recv_sem = buf, z_sem, p_sem, c_sem, recv_sem
        self.me, self.planes, self.width = me, PLANES, count // (2 * PLANES)
        self.core = me % 2
        self.spot = (me // 2) % self.width
        self.plane = me // (2 * self.width)
        self.sibling = me + 1 - 2 * self.core

    def index(self, plane, spot, core):
        return (plane * self.width + spot) * 2 + core

    def copy(self, block, send_sem, device):
        return remote(self.buf.at[block], self.buf.at[block], send_sem, self.recv_sem.at[block], device)

    def plane_at(self, step):
        half = self.planes // 2
        upper = self.plane // half
        last = self.planes - 1
        mine = self.plane + upper * (last - 2 * self.plane)
        rank = step - 1
        other = rank + (rank - mine + self.planes) // self.planes
        other = other + upper * (last - 2 * other)
        away = (step + last) // self.planes
        return self.plane + away * (other - self.plane)

    def spot_at(self, step):
        return (self.spot + step) % self.width

    def to_plane(self, block, step):
        def one(d, carry):
            device = self.index(self.plane, self.spot_at(d), self.core)
            self.copy(block, self.p_sem.at[step * (self.width - 1) + d - 1], device).start()
            return carry

        lax.fori_loop(1, self.width, one, 0)

    def to_core(self, block, slot):
        self.copy(block, self.c_sem.at[slot], self.sibling).start()

    def start(self):
        def one(d, carry):
            device = self.index(self.plane_at(d), self.spot, self.core)
            self.copy(self.me, self.z_sem.at[d - 1], device).start()
            return carry

        lax.fori_loop(1, self.planes, one, 0)
        self.to_plane(self.me, 0)
        self.to_core(self.me, 0)

    def arrived(self, block):
        self.copy(block, self.c_sem.at[0], self.sibling).wait_recv()

    def forward(self):
        def along(d, carry):
            block = self.index(self.plane_at(d), self.spot, self.core)
            self.arrived(block)
            self.to_plane(block, d)
            self.to_core(block, d)
            return carry

        lax.fori_loop(1, self.planes, along, 0)

        def within(i, carry):
            step, d = i // (self.width - 1), i % (self.width - 1) + 1
            block = self.index(self.plane_at(step), self.spot_at(d), self.core)
            self.arrived(block)
            self.to_core(block, self.planes + i)
            return carry

        lax.fori_loop(0, self.planes * (self.width - 1), within, 0)

    def finish(self):
        def last(i, carry):
            block = self.index(i // self.width, i % self.width, 1 - self.core)
            self.arrived(block)
            return carry

        lax.fori_loop(0, self.planes * self.width, last, 0)

    def drain(self):
        for sem, number in (
            (self.z_sem, self.planes - 1),
            (self.p_sem, self.planes * (self.width - 1)),
            (self.c_sem, self.planes * self.width),
        ):
            def one(i, carry, sem=sem):
                self.copy(self.me, sem.at[i], self.sibling).wait_send()
                return carry

            lax.fori_loop(0, number, one, 0)


def silu(x):
    return x * jax.nn.sigmoid(x)


def rolled_conv(values, taps, position):
    total = values * taps[0:1]
    for shift_by in range(1, CONV):
        moved = pltpu.roll(values, shift_by, 0)
        total = total + jnp.where(position >= shift_by, moved * taps[shift_by : shift_by + 1], 0.0)
    return total


def pick(row, index):
    lanes = iota(row.shape, 1)
    return jnp.sum(jnp.where(lanes == index, row, 0.0), axis=1, keepdims=True)


def split(values, number):
    parts = []
    for _ in range(number):
        part = values.astype(BF16)
        parts.append(part)
        values = values - part.astype(F32)
    return parts


def column_of(row):
    size = row.shape[1]
    same = iota((size, size), 0) == iota((size, size), 1)
    return jnp.sum(jnp.where(same, row, 0.0), axis=1, keepdims=True)


def kernel(
    count,
    hidden,
    labels,
    lengths,
    owners,
    w_inner,
    w_bcdt,
    conv_inner,
    conv_bc,
    dt_bias,
    decay_rate,
    d_skip,
    norm_gain,
    w_out,
    final_gain,
    w_head,
    layer_out,
    token_out,
    seq_out,
    h_buf,
    g_buf,
    l_buf,
    w_src,
    w_dst,
    f_buf,
    wide,
    heads,
    heads_t,
    scores,
    h_z, h_p, h_c, h_r,
    g_z, g_p, g_c, g_r,
    l_z, l_p, l_c, l_r,
    w_s, w_r,
    f_s, f_r,
    head_sem,
):
    me = lax.axis_index("blk")
    rows = hidden.shape[0]
    depth = hidden.shape[1]
    tokens = rows * count
    channels = w_inner.shape[0] // 2
    columns = depth // count
    vocab = w_head.shape[0]
    padded = heads_t.shape[0]

    fetch = pltpu.make_async_copy(w_head, heads, head_sem)
    fetch.start()
    h_buf[me] = hidden[...]

    barrier = pltpu.get_barrier_semaphore()

    def greet(d, carry):
        pl.semaphore_signal(
            barrier, inc=1, device_id={"blk": (me + d) % count}, device_id_type=pl.DeviceIdType.MESH
        )
        return carry

    lax.fori_loop(1, count, greet, 0)
    pl.semaphore_wait(barrier, count - 1)

    h_all = Gather(h_buf, h_z, h_p, h_c, h_r, count, me)
    h_all.start()

    wide[...] = w_out[...].astype(F32) * column_of(norm_gain[...])
    for e in range(count):
        w_src[e, :, 0:columns] = wide[:, e * columns : (e + 1) * columns].astype(BF16)
    h_all.forward()

    places = lengths.shape[1]
    length_row = lengths[...].astype(F32)
    length_col = column_of(length_row)
    later = iota((places, places), 0) < iota((places, places), 1)
    starts_row = jnp.sum(jnp.where(later, length_col, 0.0), axis=0, keepdims=True)
    starts_col = column_of(starts_row)
    token_row = iota((places, tokens), 1).astype(F32)
    begun = token_row >= starts_col
    start_row = jnp.max(jnp.where(begun, starts_col, 0.0), axis=0, keepdims=True)
    segment_row = jnp.sum(jnp.where(begun, 1.0, 0.0), axis=0, keepdims=True) - 1.0
    token_col = iota((tokens, places), 0).astype(F32)
    start_col = jnp.max(jnp.where(token_col >= starts_row, starts_row, 0.0), axis=1, keepdims=True)
    position = iota((tokens, 1), 0).astype(F32) - start_col

    h_all.finish()

    def give(d, carry):
        device = (me + d) % count
        remote(w_src.at[device], w_dst.at[me], w_s.at[d], w_r.at[d], device).start()
        return carry

    lax.fori_loop(1, count, give, 0)
    w_dst[me] = w_src[me]

    gathered = h_buf[...].reshape(tokens, depth)
    inner = lax.dot_general(gathered, w_inner[...], NT, preferred_element_type=F32)
    inner = inner.astype(BF16).astype(F32)
    state = lax.dot_general(gathered, w_bcdt[...], NT, preferred_element_type=F32)
    state = state.astype(BF16).astype(F32)
    gate = inner[:, :channels]
    conv_value = silu(rolled_conv(inner[:, channels:], conv_inner[...], position))
    conv_state = silu(rolled_conv(state[:, : 2 * NSTATE], conv_bc[...], position))
    raw = state[:, 2 * NSTATE :] + dt_bias[...]
    step_size = jnp.maximum(raw, 0.0) + jnp.log1p(jnp.exp(-jnp.abs(raw)))
    first = me * channels
    low = first // HEADDIM
    high = (first + channels - 1) // HEADDIM
    mask_high = (iota((1, channels), 1) + first >= high * HEADDIM).astype(F32)
    masks = (1.0 - mask_high, mask_high)
    steps = (pick(step_size, low), pick(step_size, high))
    rates = (pick(decay_rate[...], low), pick(decay_rate[...], high))
    skip = pick(d_skip[...], low) * masks[0] + pick(d_skip[...], high) * masks[1]
    driven = conv_value * (steps[0] * masks[0] + steps[1] * masks[1])
    lanes = iota((tokens, LANES), 1)
    logs = jnp.where(
        lanes == 0, -(steps[0] * rates[0]), jnp.where(lanes == 1, -(steps[1] * rates[1]), 0.0)
    )
    size = SCAN_BLOCK
    causal = iota((size, size), 0) >= iota((size, size), 1)
    lower = causal.astype(BF16)
    in_parts = split(conv_state[:, :NSTATE], 2)
    out_parts = split(conv_state[:, NSTATE:], 2)
    drive_parts = split(driven, 2)
    blocks = tokens // size
    cuts = [slice(b * size, (b + 1) * size) for b in range(blocks)]
    log_parts = split(logs, 3)
    sums_col = [
        sum(jnp.dot(lower, part[cut], preferred_element_type=F32) for part in log_parts)
        for cut in cuts
    ]
    sums_row = [jnp.transpose(s) for s in sums_col]
    results = []
    for b in range(blocks):
        result = jnp.zeros((size, channels), F32)
        for a in range(b + 1):
            gram = sum(
                lax.dot_general(
                    out_parts[i][cuts[b]], in_parts[j][cuts[a]], NT, preferred_element_type=F32
                )
                for i, j in ((0, 1), (1, 0), (0, 0))
            )
            same = start_col[cuts[b]] == start_row[:, cuts[a]]
            if a == b:
                same = same & causal
            for slot in range(2):
                rise = sums_col[b][:, slot : slot + 1]
                fall = sums_row[a][slot : slot + 1, :]
                if a == b:
                    spread = jnp.minimum(rise - fall, 0.0)
                else:
                    rest = sums_col[a][size - 1 : size, slot : slot + 1] - fall
                    for between in range(a + 1, b):
                        rest = rest + sums_col[between][size - 1 : size, slot : slot + 1]
                    spread = rise + jnp.minimum(rest, 0.0)
                weights = jnp.where(same, jnp.exp(spread), 0.0)
                mix_parts = split(gram * weights, 2)
                share = sum(
                    jnp.dot(mix_parts[i], drive_parts[j][cuts[a]], preferred_element_type=F32)
                    for i, j in ((0, 1), (1, 0), (0, 0))
                )
                result = result + share * masks[slot]
        results.append(result)
    mixed = jnp.concatenate(results, axis=0) + skip * conv_value
    gated = (mixed * silu(gate)).astype(BF16)
    eye = (iota((channels, channels), 0) == iota((channels, channels), 1)).astype(BF16)
    g_buf[me] = lax.dot_general(eye, gated, NT, preferred_element_type=F32).astype(BF16)

    g_all = Gather(g_buf, g_z, g_p, g_c, g_r, count, me)
    g_all.start()
    own_columns = (iota((columns, depth), 1) == iota((columns, depth), 0) + me * columns).astype(BF16)
    hidden_t = lax.dot_general(own_columns, gathered, NT, preferred_element_type=F32)
    g_all.forward()
    fetch.wait()
    heads_t[padded - LANES :, :] = jnp.zeros((LANES, depth), BF16)
    for k in range(depth // LANES):
        span = slice(k * LANES, (k + 1) * LANES)
        gain = final_gain[k : k + 1, :]
        heads_t[0:vocab, span] = (heads[:, span].astype(F32) * gain).astype(BF16)

    def taken(d, carry):
        device = (me + count - d) % count
        remote(w_src.at[device], w_dst.at[device], w_s.at[d], w_r.at[d], device).wait_recv()
        return carry

    lax.fori_loop(1, count, taken, 0)
    w_columns = w_dst[...].reshape(count * channels, LANES)[:, :columns]
    g_all.finish()
    g_t = g_buf[...].reshape(count * channels, tokens)
    wide_g = g_t.astype(F32)
    squares = jnp.sum(wide_g * wide_g, axis=0, keepdims=True)
    inverse = lax.rsqrt(squares / (count * channels) + EPSILON)
    delta = lax.dot_general(
        w_columns, g_t, (((0,), (0,)), ((), ())), preferred_element_type=F32
    )
    l_buf[me] = (hidden_t + delta * inverse).astype(BF16)

    l_all = Gather(l_buf, l_z, l_p, l_c, l_r, count, me)
    l_all.start()
    l_all.forward()
    l_all.finish()
    layer_t = l_buf[...].reshape(depth, tokens)
    wide_l = layer_t.astype(F32)
    scale = lax.rsqrt(jnp.sum(wide_l * wide_l, axis=0, keepdims=True) / depth + EPSILON)
    label = labels[...] - me * vocab
    top = jnp.full((1, tokens), -jnp.inf, F32)
    target = jnp.zeros((1, tokens), F32)
    for j in range(padded // LANES):
        piece = jnp.dot(
            heads_t[j * LANES : (j + 1) * LANES, :], layer_t, preferred_element_type=F32
        ) * scale
        entry = iota((LANES, tokens), 0) + j * LANES
        target = target + jnp.sum(
            jnp.where(entry == jnp.where(label < vocab, label, -1), piece, 0.0), axis=0, keepdims=True
        )
        if (j + 1) * LANES > vocab:
            piece = jnp.where(entry < vocab, piece, -jnp.inf)
        scores[j * LANES : (j + 1) * LANES, :] = piece
        top = jnp.maximum(top, jnp.max(piece, axis=0, keepdims=True))
    total = jnp.sum(jnp.exp(scores[...] - top), axis=0, keepdims=True)
    local = top + jnp.log(total)
    parts = tokens // LANES
    for i in range(parts):
        f_buf[me, i : i + 1, :] = local[:, i * LANES : (i + 1) * LANES]
        f_buf[me, parts + i : parts + i + 1, :] = target[:, i * LANES : (i + 1) * LANES]

    def tell(d, carry):
        device = (me + d) % count
        remote(f_buf.at[me], f_buf.at[me], f_s.at[d], f_r.at[d], device).start()
        return carry

    lax.fori_loop(1, count, tell, 0)

    own_rows = (iota((rows, tokens), 1) == iota((rows, tokens), 0) + me * rows).astype(BF16)
    layer_out[...] = lax.dot_general(own_rows, layer_t, NT, preferred_element_type=F32).astype(BF16)
    for gather in (h_all, g_all, l_all):
        gather.drain()

    def heard(d, carry):
        device = (me + count - d) % count
        remote(f_buf.at[device], f_buf.at[device], f_s.at[d], f_r.at[d], device).wait_recv()
        return carry

    lax.fori_loop(1, count, heard, 0)
    every = f_buf[...]
    ends = every[:, :parts, :]
    peak = jnp.max(ends, axis=0)
    norm = peak + jnp.log(jnp.sum(jnp.exp(ends - peak[None]), axis=0))
    square = jnp.sum(every[:, parts:, :], axis=0) - norm
    logprob = jnp.concatenate([square[i : i + 1, :] for i in range(parts)], axis=1)
    token_out[...] = lax.dot_general(
        jnp.broadcast_to(logprob, (8, tokens)), own_rows.astype(F32), NT, precision=HIGH
    )[0:1, :]
    member = iota((places, tokens), 0).astype(F32) == segment_row
    sums = jnp.sum(jnp.where(member, logprob, 0.0), axis=1, keepdims=True)
    owner_col = column_of(owners[...].astype(F32))
    slots = iota((places, places), 1).astype(F32) == owner_col
    seq_out[...] = jnp.sum(jnp.where(slots, sums, 0.0), axis=0, keepdims=True)

    def sent(d, carry):
        remote(w_src.at[me], w_dst.at[me], w_s.at[d], w_r.at[d], h_all.sibling).wait_send()
        remote(f_buf.at[me], f_buf.at[me], f_s.at[d], f_r.at[d], h_all.sibling).wait_send()
        return carry

    lax.fori_loop(1, count, sent, 0)


def fused(
    hidden,
    labels,
    lengths,
    owners,
    w_inner,
    w_bcdt,
    conv_inner,
    conv_bc,
    dt_bias,
    decay_rate,
    d_skip,
    norm_gain,
    w_out,
    final_gain,
    w_head,
):
    count = lax.axis_size("blk")
    rows, depth = hidden.shape[1:]
    tokens = rows * count
    channels = w_inner.shape[2]
    vocab = w_head.shape[1]
    padded = -(-vocab // LANES) * LANES
    width = count // (2 * PLANES)
    vmem = pl.BlockSpec(memory_space=pltpu.VMEM)
    gather_sems = [
        pltpu.SemaphoreType.DMA((PLANES - 1,)),
        pltpu.SemaphoreType.DMA((PLANES * (width - 1),)),
        pltpu.SemaphoreType.DMA((PLANES * width,)),
        pltpu.SemaphoreType.DMA((count,)),
    ]
    layer, token, seq = pl.pallas_call(
        functools.partial(kernel, count),
        out_shape=(
            jax.ShapeDtypeStruct((rows, depth), BF16),
            jax.ShapeDtypeStruct((1, rows), F32),
            jax.ShapeDtypeStruct((1, owners.shape[0]), F32),
        ),
        in_specs=[vmem] * 14 + [pl.BlockSpec(memory_space=pl.ANY)],
        out_specs=(vmem, vmem, vmem),
        scratch_shapes=[
            pltpu.VMEM((count, rows, depth), BF16),
            pltpu.VMEM((count, channels, tokens), BF16),
            pltpu.VMEM((count, depth // count, tokens), BF16),
            pltpu.VMEM((count, channels, LANES), BF16),
            pltpu.VMEM((count, channels, LANES), BF16),
            pltpu.VMEM((count, 2 * tokens // LANES, LANES), F32),
            pltpu.VMEM((channels, depth), F32),
            pltpu.VMEM((vocab, depth), BF16),
            pltpu.VMEM((padded, depth), BF16),
            pltpu.VMEM((padded, tokens), F32),
        ]
        + gather_sems * 3
        + [pltpu.SemaphoreType.DMA((count,))] * 4
        + [pltpu.SemaphoreType.DMA],
        compiler_params=pltpu.CompilerParams(
            collective_id=0, has_side_effects=True, vmem_limit_bytes=56 * 1024 * 1024
        ),
    )(
        hidden[0],
        labels,
        lengths,
        owners.reshape(1, -1),
        w_inner.transpose(1, 2, 0).reshape(2 * channels, depth),
        w_bcdt.T,
        conv_inner,
        conv_bc,
        dt_bias.reshape(1, -1),
        decay_rate.reshape(1, -1),
        d_skip.reshape(1, -1),
        norm_gain.reshape(1, -1),
        w_out,
        final_gain.reshape(-1, LANES),
        w_head.T,
    )
    return (layer[None], token, seq[0])


def layer(*args):
    hidden, w_inner = args[0], args[4]
    count = lax.axis_size("blk")
    rows, depth = hidden.shape[1:]
    tokens = rows * count
    whole = lax.axis_size("seq") == 1 and count % (4 * PLANES) == 0
    tiled = rows % 16 == 0 and w_inner.shape[2] % 16 == 0 and depth % (16 * count) == 0
    sized = depth // count <= LANES and tokens % SCAN_BLOCK == 0 and depth % LANES == 0
    return (fused if whole and tiled and sized else shards)(*args)


def solution(mesh):
    in_specs = (
        P(("mp", "seq"), "blk", None),
        P("seq", None),
        P("seq", None),
        P(),
        P("mp", None, "blk"),
        P("mp", None),
        P("mp", "blk"),
        P("mp", None),
        P("mp"),
        P("mp"),
        P("mp"),
        P(("mp", "blk")),
        P(("mp", "blk"), None),
        P("mp"),
        P("mp", "blk"),
    )
    out_specs = (P(("mp", "seq"), "blk", None), P(("mp", "seq"), "blk"), P(("mp", "seq")))
    return jax.shard_map(layer, mesh=mesh, in_specs=in_specs, out_specs=out_specs, check_vma=False)
```

```python
import functools

import jax
import jax.numpy as jnp
from jax import lax
from jax.experimental import pallas as pl
from jax.experimental.pallas import tpu as pltpu
from jax.sharding import PartitionSpec as P

D = 1536
HEADDIM = 64
NSTATE = 128
SCAN_BLOCK = 256
CONV = 4


EPSILON = 1e-05
HIGH = lax.Precision.HIGHEST


def segments_of(lengths, count):
    order = jnp.arange(lengths.shape[0], dtype=jnp.int32)
    earlier = order[None, :] < order[:, None]
    starts = jnp.sum(jnp.where(earlier, lengths[None, :], 0), axis=-1)
    places = jnp.arange(count, dtype=jnp.int32)
    segment = jnp.sum((places[:, None] >= starts[None, :]).astype(jnp.int32), axis=-1) - 1
    first = jnp.take(starts, segment)
    return (segment, places - first)


def causal_conv(values, weights, position):
    total = values * weights[0]
    for shift_by in range(1, CONV):
        moved = jnp.concatenate(
            [jnp.zeros_like(values[:shift_by, :]), values[:-shift_by, :]], axis=0
        )
        total = (
            total + moved * weights[shift_by] * (position >= shift_by).astype(jnp.float32)[:, None]
        )
    return total


def final_norm(values, gain):
    widened = values.astype(jnp.float32)
    scale = lax.rsqrt(jnp.mean(widened * widened, axis=-1, keepdims=True) + EPSILON)
    return (widened * scale * gain).astype(jnp.bfloat16)


def shards(
    hidden,
    labels,
    lengths,
    owners,
    w_inner,
    w_bcdt,
    conv_inner,
    conv_bc,
    dt_bias,
    decay_rate,
    d_skip,
    norm_gain,
    w_out,
    final_gain,
    w_head,
):
    rows_own = hidden[0]
    rows_count = rows_own.shape[0]
    blk_count = lax.axis_size("blk")
    blk_index = lax.axis_index("blk")
    gathered = lax.all_gather(rows_own, "blk", axis=0, tiled=True)
    tokens_all = gathered.shape[0]
    channels = w_inner.shape[2]
    inner_total = channels * blk_count
    inner_proj = jnp.dot(
        gathered, w_inner.reshape(D, 2 * channels), preferred_element_type=jnp.float32
    ).astype(jnp.bfloat16)
    state_proj = jnp.dot(gathered, w_bcdt, preferred_element_type=jnp.float32).astype(jnp.bfloat16)
    gate_half = inner_proj[:, :channels].astype(jnp.float32)
    segment, position = segments_of(lengths[0], tokens_all)
    conv_value = jax.nn.silu(
        causal_conv(inner_proj[:, channels:].astype(jnp.float32), conv_inner, position)
    )
    conv_state = jax.nn.silu(
        causal_conv(state_proj[:, : 2 * NSTATE].astype(jnp.float32), conv_bc, position)
    )
    input_map = conv_state[:, :NSTATE]
    output_map = conv_state[:, NSTATE:]
    step_size = jax.nn.softplus(state_proj[:, 2 * NSTATE :].astype(jnp.float32) + dt_bias)
    log_heads = -(step_size * decay_rate)
    first_channel = blk_index * channels
    channel_head = (first_channel + jnp.arange(channels, dtype=jnp.int32)) // HEADDIM
    head_low = first_channel // HEADDIM
    head_high = (first_channel + channels - 1) // HEADDIM
    mask_high = (channel_head == head_high).astype(jnp.float32)
    mask_low = 1.0 - mask_high
    step_pair = jnp.concatenate(
        [
            lax.dynamic_slice_in_dim(step_size, head_low, 1, 1),
            lax.dynamic_slice_in_dim(step_size, head_high, 1, 1),
        ],
        axis=1,
    )
    log_pair = jnp.concatenate(
        [
            lax.dynamic_slice_in_dim(log_heads, head_low, 1, 1),
            lax.dynamic_slice_in_dim(log_heads, head_high, 1, 1),
        ],
        axis=1,
    )
    step_channel = step_pair[:, 0:1] * mask_low + step_pair[:, 1:2] * mask_high
    driven = conv_value * step_channel
    slot_masks = (mask_low, mask_high)
    blocks = tokens_all // SCAN_BLOCK
    order = jnp.arange(SCAN_BLOCK, dtype=jnp.int32)
    causal = order[:, None] >= order[None, :]

    def block_step(carry, inputs):
        carried, previous = carry
        drive_block, in_block, out_block, log_block, seg_block = inputs
        cumulative = jnp.dot(causal.astype(jnp.float32), log_block, precision=HIGH)
        gram = jnp.dot(out_block, in_block.T, precision=HIGH)
        same = (seg_block[:, None] == seg_block[None, :]) & causal
        result = jnp.zeros((SCAN_BLOCK, channels), jnp.float32)
        for slot_index in range(2):
            column = cumulative[:, slot_index]
            spread = jnp.minimum(column[:, None] - column[None, :], 0.0)
            weights = jnp.where(same, jnp.exp(spread), 0.0)
            result = result + jnp.dot(
                gram * weights, drive_block * slot_masks[slot_index], precision=HIGH
            )
        carried_in = carried * (seg_block[0] == previous).astype(jnp.float32)
        rising = jnp.exp(cumulative[:, 0:1]) * mask_low + jnp.exp(cumulative[:, 1:2]) * mask_high
        leading = (seg_block == seg_block[0]).astype(jnp.float32)[:, None]
        result = result + leading * rising * jnp.dot(out_block, carried_in.T, precision=HIGH)
        trailing = (seg_block == seg_block[-1]).astype(jnp.float32)[:, None]
        tail_low = jnp.exp(cumulative[-1:, 0:1] - cumulative[:, 0:1])
        tail_high = jnp.exp(cumulative[-1:, 1:2] - cumulative[:, 1:2])
        tail = tail_low * mask_low + tail_high * mask_high
        whole_block = (seg_block[-1] == seg_block[0]).astype(jnp.float32)
        carried_new = whole_block * rising[-1][:, None] * carried_in + jnp.dot(
            (drive_block * tail * trailing).T, in_block, precision=HIGH
        )
        return ((carried_new, seg_block[-1]), result)

    initial = (jnp.zeros((channels, NSTATE), jnp.float32), jnp.int32(-1))
    scan_inputs = (
        driven.reshape(blocks, SCAN_BLOCK, channels),
        input_map.reshape(blocks, SCAN_BLOCK, NSTATE),
        output_map.reshape(blocks, SCAN_BLOCK, NSTATE),
        log_pair.reshape(blocks, SCAN_BLOCK, 2),
        segment.reshape(blocks, SCAN_BLOCK),
    )
    final_carry, scanned = lax.scan(block_step, initial, scan_inputs)
    mixed = scanned.reshape(tokens_all, channels) + jnp.take(d_skip, channel_head) * conv_value
    gated = mixed * jax.nn.silu(gate_half)
    squares = lax.psum(jnp.sum(gated * gated, axis=1), "blk")
    inverse = lax.rsqrt(squares / inner_total + EPSILON)
    gated_norm = (gated * inverse[:, None] * norm_gain).astype(jnp.bfloat16)
    delta_own = lax.psum_scatter(
        jnp.dot(gated_norm, w_out, preferred_element_type=jnp.float32),
        "blk",
        scatter_dimension=0,
        tiled=True,
    )
    layer_own = (rows_own.astype(jnp.float32) + delta_own).astype(jnp.bfloat16)
    logits = jnp.dot(
        lax.all_gather(final_norm(layer_own, final_gain), "blk", axis=0, tiled=True),
        w_head,
        preferred_element_type=jnp.float32,
    )
    vocab_local = w_head.shape[1]
    local_label = labels[0] - blk_index * vocab_local
    hit = jnp.arange(vocab_local, dtype=jnp.int32)[None, :] == local_label[:, None]
    target_local = jnp.sum(jnp.where(hit, logits, 0.0), axis=1)
    top_local = jnp.max(logits, axis=1)
    top_all = lax.pmax(top_local, "blk")
    expsum_local = jnp.sum(jnp.exp(logits - top_all[:, None]), axis=1)
    expsum_all, target_all = lax.psum((expsum_local, target_local), "blk")
    logprob = target_all - (top_all + jnp.log(expsum_all))
    token_own = lax.dynamic_slice_in_dim(logprob, blk_index * rows_count, rows_count, 0)
    seqs_count = lengths.shape[1]
    onehot = (segment[:, None] == jnp.arange(seqs_count, dtype=jnp.int32)[None, :]).astype(
        jnp.float32
    )
    sums = jnp.dot(logprob, onehot, precision=HIGH)
    seq_index = lax.axis_index("seq")
    mine = lax.dynamic_slice_in_dim(owners, seq_index * seqs_count, seqs_count, 0)
    placement = (mine[:, None] == jnp.arange(owners.shape[0], dtype=jnp.int32)[None, :]).astype(
        jnp.float32
    )
    spread_sums = jnp.dot(sums, placement, precision=HIGH)
    seq_own = lax.psum_scatter(spread_sums, "seq", scatter_dimension=0, tiled=True)
    return (layer_own[None], token_own[None], seq_own)


LANES = 128
PLANES = 4
NT = (((1,), (1,)), ((), ()))
F32 = jnp.float32
BF16 = jnp.bfloat16


def iota(shape, dim):
    return lax.broadcasted_iota(jnp.int32, shape, dim)


def remote(source, target, send_sem, recv_sem, device):
    return pltpu.make_async_remote_copy(
        src_ref=source,
        dst_ref=target,
        send_sem=send_sem,
        recv_sem=recv_sem,
        device_id={"blk": device},
        device_id_type=pl.DeviceIdType.MESH,
    )


class Gather:
    def __init__(self, buf, z_sem, p_sem, c_sem, recv_sem, count, me):
        self.buf, self.z_sem, self.p_sem, self.c_sem, self.recv_sem = buf, z_sem, p_sem, c_sem, recv_sem
        self.me, self.planes, self.width = me, PLANES, count // (2 * PLANES)
        self.core = me % 2
        self.spot = (me // 2) % self.width
        self.plane = me // (2 * self.width)
        self.sibling = me + 1 - 2 * self.core

    def index(self, plane, spot, core):
        return (plane * self.width + spot) * 2 + core

    def copy(self, block, send_sem, device):
        return remote(self.buf.at[block], self.buf.at[block], send_sem, self.recv_sem.at[block], device)

    def plane_at(self, step):
        half = self.planes // 2
        upper = self.plane // half
        last = self.planes - 1
        mine = self.plane + upper * (last - 2 * self.plane)
        rank = step - 1
        other = rank + (rank - mine + self.planes) // self.planes
        other = other + upper * (last - 2 * other)
        away = (step + last) // self.planes
        return self.plane + away * (other - self.plane)

    def beside(self, d):
        x, y = self.spot % 2, self.spot // 2
        along_x, along_y = self.spot + 1 - 2 * x, self.spot + 2 - 4 * y
        first = along_x + self.core * (along_y - along_x)
        return (first, along_x + along_y - first, self.width - 1 - self.spot)[d]

    def to_plane(self, block, step):
        for d in range(2):
            device = self.index(self.plane, self.beside(d), self.core)
            self.copy(block, self.p_sem.at[step * (self.width - 1) + d], device).start()

    def to_core(self, block, slot):
        self.copy(block, self.c_sem.at[slot], self.sibling).start()

    def start(self):
        def one(d, carry):
            device = self.index(self.plane_at(d), self.spot, self.core)
            self.copy(self.me, self.z_sem.at[d - 1], device).start()
            return carry

        lax.fori_loop(1, self.planes, one, 0)
        self.to_plane(self.me, 0)
        self.to_core(self.me, 0)

    def arrived(self, block):
        self.copy(block, self.c_sem.at[0], self.sibling).wait_recv()

    def receive(self, step, d):
        block = self.index(self.plane_at(step), self.beside(d), self.core)
        self.arrived(block)
        slot = step * (self.width - 1) + d
        if d == 0:
            device = self.index(self.plane, self.beside(1), self.core)
            self.copy(block, self.p_sem.at[step * (self.width - 1) + 2], device).start()
        self.to_core(block, self.planes + slot)

    def forward(self):
        def along(step, carry):
            block = self.index(self.plane_at(step), self.spot, self.core)
            self.arrived(block)
            self.to_plane(block, step)
            self.to_core(block, step)
            self.receive(step - 1, 0)
            self.receive(step - 1, 1)
            return carry

        lax.fori_loop(1, self.planes, along, 0)
        self.receive(self.planes - 1, 0)
        self.receive(self.planes - 1, 1)

        def across(step, carry):
            self.receive(step, 2)
            return carry

        lax.fori_loop(0, self.planes, across, 0)

    def finish(self):
        def last(i, carry):
            block = self.index(i // self.width, i % self.width, 1 - self.core)
            self.arrived(block)
            return carry

        lax.fori_loop(0, self.planes * self.width, last, 0)

    def drain(self):
        for sem, number in (
            (self.z_sem, self.planes - 1),
            (self.p_sem, self.planes * (self.width - 1)),
            (self.c_sem, self.planes * self.width),
        ):
            def one(i, carry, sem=sem):
                self.copy(self.me, sem.at[i], self.sibling).wait_send()
                return carry

            lax.fori_loop(0, number, one, 0)


def silu(x):
    return x * jax.nn.sigmoid(x)


def rolled_conv(values, taps, position):
    total = values * taps[0:1]
    for shift_by in range(1, CONV):
        moved = pltpu.roll(values, shift_by, 0)
        total = total + jnp.where(position >= shift_by, moved * taps[shift_by : shift_by + 1], 0.0)
    return total


def pick(row, index):
    lanes = iota(row.shape, 1)
    return jnp.sum(jnp.where(lanes == index, row, 0.0), axis=1, keepdims=True)


def split(values, number):
    parts = []
    for _ in range(number):
        part = values.astype(BF16)
        parts.append(part)
        values = values - part.astype(F32)
    return parts


def column_of(row):
    size = row.shape[1]
    same = iota((size, size), 0) == iota((size, size), 1)
    return jnp.sum(jnp.where(same, row, 0.0), axis=1, keepdims=True)


def kernel(
    count,
    hidden,
    labels,
    lengths,
    owners,
    w_inner,
    w_bcdt,
    conv_inner,
    conv_bc,
    dt_bias,
    decay_rate,
    d_skip,
    norm_gain,
    w_out,
    final_gain,
    w_head,
    layer_out,
    token_out,
    seq_out,
    h_buf,
    g_buf,
    l_buf,
    w_src,
    w_dst,
    f_buf,
    wide,
    heads,
    heads_t,
    scores,
    h_z, h_p, h_c, h_r,
    g_z, g_p, g_c, g_r,
    l_z, l_p, l_c, l_r,
    w_s, w_r,
    f_s, f_r,
    head_sem,
):
    me = lax.axis_index("blk")
    rows = hidden.shape[0]
    depth = hidden.shape[1]
    tokens = rows * count
    channels = w_inner.shape[0] // 2
    columns = depth // count
    vocab = w_head.shape[0]
    padded = heads_t.shape[0]

    fetch = pltpu.make_async_copy(w_head, heads, head_sem)
    fetch.start()
    h_buf[me] = hidden[...]

    barrier = pltpu.get_barrier_semaphore()

    def greet(d, carry):
        pl.semaphore_signal(
            barrier, inc=1, device_id={"blk": (me + d) % count}, device_id_type=pl.DeviceIdType.MESH
        )
        return carry

    lax.fori_loop(1, count, greet, 0)
    pl.semaphore_wait(barrier, count - 1)

    h_all = Gather(h_buf, h_z, h_p, h_c, h_r, count, me)
    h_all.start()

    wide[...] = w_out[...].astype(F32) * column_of(norm_gain[...])
    for e in range(count):
        w_src[e, :, 0:columns] = wide[:, e * columns : (e + 1) * columns].astype(BF16)
    h_all.forward()

    places = lengths.shape[1]
    length_row = lengths[...].astype(F32)
    length_col = column_of(length_row)
    later = iota((places, places), 0) < iota((places, places), 1)
    starts_row = jnp.sum(jnp.where(later, length_col, 0.0), axis=0, keepdims=True)
    starts_col = column_of(starts_row)
    token_row = iota((places, tokens), 1).astype(F32)
    begun = token_row >= starts_col
    start_row = jnp.max(jnp.where(begun, starts_col, 0.0), axis=0, keepdims=True)
    segment_row = jnp.sum(jnp.where(begun, 1.0, 0.0), axis=0, keepdims=True) - 1.0
    token_col = iota((tokens, places), 0).astype(F32)
    start_col = jnp.max(jnp.where(token_col >= starts_row, starts_row, 0.0), axis=1, keepdims=True)
    position = iota((tokens, 1), 0).astype(F32) - start_col

    h_all.finish()

    def give(d, carry):
        device = (me + d) % count
        remote(w_src.at[device], w_dst.at[me], w_s.at[d], w_r.at[d], device).start()
        return carry

    lax.fori_loop(1, count, give, 0)
    w_dst[me] = w_src[me]

    gathered = h_buf[...].reshape(tokens, depth)
    inner = lax.dot_general(gathered, w_inner[...], NT, preferred_element_type=F32)
    inner = inner.astype(BF16).astype(F32)
    state = lax.dot_general(gathered, w_bcdt[...], NT, preferred_element_type=F32)
    state = state.astype(BF16).astype(F32)
    gate = inner[:, :channels]
    conv_value = silu(rolled_conv(inner[:, channels:], conv_inner[...], position))
    conv_state = silu(rolled_conv(state[:, : 2 * NSTATE], conv_bc[...], position))
    raw = state[:, 2 * NSTATE :] + dt_bias[...]
    step_size = jnp.maximum(raw, 0.0) + jnp.log1p(jnp.exp(-jnp.abs(raw)))
    first = me * channels
    low = first // HEADDIM
    high = (first + channels - 1) // HEADDIM
    mask_high = (iota((1, channels), 1) + first >= high * HEADDIM).astype(F32)
    masks = (1.0 - mask_high, mask_high)
    steps = (pick(step_size, low), pick(step_size, high))
    rates = (pick(decay_rate[...], low), pick(decay_rate[...], high))
    skip = pick(d_skip[...], low) * masks[0] + pick(d_skip[...], high) * masks[1]
    driven = conv_value * (steps[0] * masks[0] + steps[1] * masks[1])
    lanes = iota((tokens, LANES), 1)
    logs = jnp.where(
        lanes == 0, -(steps[0] * rates[0]), jnp.where(lanes == 1, -(steps[1] * rates[1]), 0.0)
    )
    size = SCAN_BLOCK
    causal = iota((size, size), 0) >= iota((size, size), 1)
    lower = causal.astype(BF16)
    in_parts = split(conv_state[:, :NSTATE], 2)
    out_parts = split(conv_state[:, NSTATE:], 2)
    drive_parts = split(driven, 2)
    blocks = tokens // size
    cuts = [slice(b * size, (b + 1) * size) for b in range(blocks)]
    log_parts = split(logs, 3)
    sums_col = [
        sum(jnp.dot(lower, part[cut], preferred_element_type=F32) for part in log_parts)
        for cut in cuts
    ]
    sums_row = [jnp.transpose(s) for s in sums_col]
    results = []
    for b in range(blocks):
        result = jnp.zeros((size, channels), F32)
        for a in range(b + 1):
            gram = sum(
                lax.dot_general(
                    out_parts[i][cuts[b]], in_parts[j][cuts[a]], NT, preferred_element_type=F32
                )
                for i, j in ((0, 1), (1, 0), (0, 0))
            )
            same = start_col[cuts[b]] == start_row[:, cuts[a]]
            if a == b:
                same = same & causal
            for slot in range(2):
                rise = sums_col[b][:, slot : slot + 1]
                fall = sums_row[a][slot : slot + 1, :]
                if a == b:
                    spread = jnp.minimum(rise - fall, 0.0)
                else:
                    rest = sums_col[a][size - 1 : size, slot : slot + 1] - fall
                    for between in range(a + 1, b):
                        rest = rest + sums_col[between][size - 1 : size, slot : slot + 1]
                    spread = rise + jnp.minimum(rest, 0.0)
                weights = jnp.where(same, jnp.exp(spread), 0.0)
                mix_parts = split(gram * weights, 2)
                share = sum(
                    jnp.dot(mix_parts[i], drive_parts[j][cuts[a]], preferred_element_type=F32)
                    for i, j in ((0, 1), (1, 0), (0, 0))
                )
                result = result + share * masks[slot]
        results.append(result)
    mixed = jnp.concatenate(results, axis=0) + skip * conv_value
    gated = (mixed * silu(gate)).astype(BF16)
    eye = (iota((channels, channels), 0) == iota((channels, channels), 1)).astype(BF16)
    g_buf[me] = lax.dot_general(eye, gated, NT, preferred_element_type=F32).astype(BF16)

    g_all = Gather(g_buf, g_z, g_p, g_c, g_r, count, me)
    g_all.start()
    own_columns = (iota((columns, depth), 1) == iota((columns, depth), 0) + me * columns).astype(BF16)
    hidden_t = lax.dot_general(own_columns, gathered, NT, preferred_element_type=F32)
    g_all.forward()
    fetch.wait()
    heads_t[padded - LANES :, :] = jnp.zeros((LANES, depth), BF16)
    for k in range(depth // LANES):
        span = slice(k * LANES, (k + 1) * LANES)
        gain = final_gain[k : k + 1, :]
        heads_t[0:vocab, span] = (heads[:, span].astype(F32) * gain).astype(BF16)

    def taken(d, carry):
        device = (me + count - d) % count
        remote(w_src.at[device], w_dst.at[device], w_s.at[d], w_r.at[d], device).wait_recv()
        return carry

    lax.fori_loop(1, count, taken, 0)
    w_columns = w_dst[...].reshape(count * channels, LANES)[:, :columns]
    g_all.finish()
    g_t = g_buf[...].reshape(count * channels, tokens)
    wide_g = g_t.astype(F32)
    squares = jnp.sum(wide_g * wide_g, axis=0, keepdims=True)
    inverse = lax.rsqrt(squares / (count * channels) + EPSILON)
    delta = lax.dot_general(
        w_columns, g_t, (((0,), (0,)), ((), ())), preferred_element_type=F32
    )
    l_buf[me] = (hidden_t + delta * inverse).astype(BF16)

    l_all = Gather(l_buf, l_z, l_p, l_c, l_r, count, me)
    l_all.start()
    l_all.forward()
    l_all.finish()
    layer_t = l_buf[...].reshape(depth, tokens)
    wide_l = layer_t.astype(F32)
    scale = lax.rsqrt(jnp.sum(wide_l * wide_l, axis=0, keepdims=True) / depth + EPSILON)
    label = labels[...] - me * vocab
    top = jnp.full((1, tokens), -jnp.inf, F32)
    target = jnp.zeros((1, tokens), F32)
    for j in range(padded // LANES):
        piece = jnp.dot(
            heads_t[j * LANES : (j + 1) * LANES, :], layer_t, preferred_element_type=F32
        ) * scale
        entry = iota((LANES, tokens), 0) + j * LANES
        target = target + jnp.sum(
            jnp.where(entry == jnp.where(label < vocab, label, -1), piece, 0.0), axis=0, keepdims=True
        )
        if (j + 1) * LANES > vocab:
            piece = jnp.where(entry < vocab, piece, -jnp.inf)
        scores[j * LANES : (j + 1) * LANES, :] = piece
        top = jnp.maximum(top, jnp.max(piece, axis=0, keepdims=True))
    total = jnp.sum(jnp.exp(scores[...] - top), axis=0, keepdims=True)
    local = top + jnp.log(total)
    parts = tokens // LANES
    for i in range(parts):
        f_buf[me, i : i + 1, :] = local[:, i * LANES : (i + 1) * LANES]
        f_buf[me, parts + i : parts + i + 1, :] = target[:, i * LANES : (i + 1) * LANES]

    def tell(d, carry):
        device = (me + d) % count
        remote(f_buf.at[me], f_buf.at[me], f_s.at[d], f_r.at[d], device).start()
        return carry

    lax.fori_loop(1, count, tell, 0)

    own_rows = (iota((rows, tokens), 1) == iota((rows, tokens), 0) + me * rows).astype(BF16)
    layer_out[...] = lax.dot_general(own_rows, layer_t, NT, preferred_element_type=F32).astype(BF16)
    for gather in (h_all, g_all, l_all):
        gather.drain()

    def heard(d, carry):
        device = (me + count - d) % count
        remote(f_buf.at[device], f_buf.at[device], f_s.at[d], f_r.at[d], device).wait_recv()
        return carry

    lax.fori_loop(1, count, heard, 0)
    every = f_buf[...]
    ends = every[:, :parts, :]
    peak = jnp.max(ends, axis=0)
    norm = peak + jnp.log(jnp.sum(jnp.exp(ends - peak[None]), axis=0))
    square = jnp.sum(every[:, parts:, :], axis=0) - norm
    logprob = jnp.concatenate([square[i : i + 1, :] for i in range(parts)], axis=1)
    token_out[...] = lax.dot_general(
        jnp.broadcast_to(logprob, (8, tokens)), own_rows.astype(F32), NT, precision=HIGH
    )[0:1, :]
    member = iota((places, tokens), 0).astype(F32) == segment_row
    sums = jnp.sum(jnp.where(member, logprob, 0.0), axis=1, keepdims=True)
    owner_col = column_of(owners[...].astype(F32))
    slots = iota((places, places), 1).astype(F32) == owner_col
    seq_out[...] = jnp.sum(jnp.where(slots, sums, 0.0), axis=0, keepdims=True)

    def sent(d, carry):
        remote(w_src.at[me], w_dst.at[me], w_s.at[d], w_r.at[d], h_all.sibling).wait_send()
        remote(f_buf.at[me], f_buf.at[me], f_s.at[d], f_r.at[d], h_all.sibling).wait_send()
        return carry

    lax.fori_loop(1, count, sent, 0)


def fused(
    hidden,
    labels,
    lengths,
    owners,
    w_inner,
    w_bcdt,
    conv_inner,
    conv_bc,
    dt_bias,
    decay_rate,
    d_skip,
    norm_gain,
    w_out,
    final_gain,
    w_head,
):
    count = lax.axis_size("blk")
    rows, depth = hidden.shape[1:]
    tokens = rows * count
    channels = w_inner.shape[2]
    vocab = w_head.shape[1]
    padded = -(-vocab // LANES) * LANES
    width = count // (2 * PLANES)
    vmem = pl.BlockSpec(memory_space=pltpu.VMEM)
    gather_sems = [
        pltpu.SemaphoreType.DMA((PLANES - 1,)),
        pltpu.SemaphoreType.DMA((PLANES * (width - 1),)),
        pltpu.SemaphoreType.DMA((PLANES * width,)),
        pltpu.SemaphoreType.DMA((count,)),
    ]
    layer, token, seq = pl.pallas_call(
        functools.partial(kernel, count),
        out_shape=(
            jax.ShapeDtypeStruct((rows, depth), BF16),
            jax.ShapeDtypeStruct((1, rows), F32),
            jax.ShapeDtypeStruct((1, owners.shape[0]), F32),
        ),
        in_specs=[vmem] * 14 + [pl.BlockSpec(memory_space=pl.ANY)],
        out_specs=(vmem, vmem, vmem),
        scratch_shapes=[
            pltpu.VMEM((count, rows, depth), BF16),
            pltpu.VMEM((count, channels, tokens), BF16),
            pltpu.VMEM((count, depth // count, tokens), BF16),
            pltpu.VMEM((count, channels, LANES), BF16),
            pltpu.VMEM((count, channels, LANES), BF16),
            pltpu.VMEM((count, 2 * tokens // LANES, LANES), F32),
            pltpu.VMEM((channels, depth), F32),
            pltpu.VMEM((vocab, depth), BF16),
            pltpu.VMEM((padded, depth), BF16),
            pltpu.VMEM((padded, tokens), F32),
        ]
        + gather_sems * 3
        + [pltpu.SemaphoreType.DMA((count,))] * 4
        + [pltpu.SemaphoreType.DMA],
        compiler_params=pltpu.CompilerParams(
            collective_id=0, has_side_effects=True, vmem_limit_bytes=56 * 1024 * 1024
        ),
    )(
        hidden[0],
        labels,
        lengths,
        owners.reshape(1, -1),
        w_inner.transpose(1, 2, 0).reshape(2 * channels, depth),
        w_bcdt.T,
        conv_inner,
        conv_bc,
        dt_bias.reshape(1, -1),
        decay_rate.reshape(1, -1),
        d_skip.reshape(1, -1),
        norm_gain.reshape(1, -1),
        w_out,
        final_gain.reshape(-1, LANES),
        w_head.T,
    )
    return (layer[None], token, seq[0])


def layer(*args):
    hidden, w_inner = args[0], args[4]
    count = lax.axis_size("blk")
    rows, depth = hidden.shape[1:]
    tokens = rows * count
    whole = lax.axis_size("seq") == 1 and count == 8 * PLANES
    tiled = rows % 16 == 0 and w_inner.shape[2] % 16 == 0 and depth % (16 * count) == 0
    sized = depth // count <= LANES and tokens % SCAN_BLOCK == 0 and depth % LANES == 0
    return (fused if whole and tiled and sized else shards)(*args)


def solution(mesh):
    in_specs = (
        P(("mp", "seq"), "blk", None),
        P("seq", None),
        P("seq", None),
        P(),
        P("mp", None, "blk"),
        P("mp", None),
        P("mp", "blk"),
        P("mp", None),
        P("mp"),
        P("mp"),
        P("mp"),
        P(("mp", "blk")),
        P(("mp", "blk"), None),
        P("mp"),
        P("mp", "blk"),
    )
    out_specs = (P(("mp", "seq"), "blk", None), P(("mp", "seq"), "blk"), P(("mp", "seq")))
    return jax.shard_map(layer, mesh=mesh, in_specs=in_specs, out_specs=out_specs, check_vma=False)
```
